32 devices in a mesh: mu: 8 (over y, x, core), aux: 4 (over z).
Axes of the slice: x: 2, y: 2, z: 4, core: 2. Of those that a mesh axis runs over, the one named last changes fastest.
Arguments:
- b_tensor: bfloat16 [64, 512, 512], P('aux', 'mu'), as said below
- density: bfloat16 [512, 512], P('mu'), may hold values from -0.25 to 0.25
- pair_mask: int32 [8, 8], replicated, may hold values from 0 to 1, as said below
- dens_mask: int32 [8, 8], replicated, may hold values from 0 to 1, as said below
Outputs:
- exchange_k: float32 [512, 512], P(('mu', 'aux'))
The draws below stay inside these ranges and needn't reach their ends.
Inputs may be any that keep to these rules, and one draw needn't show every extreme that they name: `pair_mask`: symmetric, with ones on the diagonal. `dens_mask`: symmetric, with ones on the diagonal. `b_tensor`: symmetric in its last two dimensions.
All inputs are finite; a program needn't handle non-finite values.
Results may differ from the reference program's by a relative error of at most 0.0029.
Values may be sent and summed in bfloat16 or wider, within the bound.
No kernel may reach another device: no remote copies, remote signals or barrier semaphores. Data moves between devices by JAX's collectives and lax.ppermute only.
A program may use at most 128 MiB of HBM per device.

```python
import jax
import jax.numpy as jnp
from jax import lax

BLK = 64
NB = 8
NBAS = 512
PA = 64


def local_mask(key, salt, reach):
    first, second = jax.random.split(jax.random.fold_in(key, salt))
    index = jnp.arange(NB)
    row = index[:, None]
    col = index[None, :]
    gap = jnp.abs(row - col)
    gap = jnp.minimum(gap, NB - gap)
    weight = jax.random.randint(first, (NB,), 1, 4)
    load = jnp.maximum(weight[:, None], weight[None, :])
    limit = jnp.maximum(100 - gap * reach // load, 12)
    rolls = jax.random.randint(second, (NB, NB), 0, 100)
    rolls = jnp.where(row <= col, rolls, rolls.T)
    keep = (rolls < limit) | (row == col)
    return keep.astype(jnp.int32)


def draw_pair_mask(key, part):
    return local_mask(key, 17, 60)


def draw_dens_mask(key, part):
    return local_mask(key, 29, 30)


def draw_b_tensor(key, part):
    first = jax.random.fold_in(jax.random.fold_in(key, 41), 0)
    scale = 1.4 * (PA * NBAS) ** (-0.25)
    base = jax.random.normal(first, (PA, NBAS, NBAS), jnp.float32)
    sym = (base + jnp.swapaxes(base, 1, 2)) * (0.7071 * scale)
    return sym.astype(jnp.bfloat16)


def block_levels(stream_key, dims, cuts, smallest, largest):
    loudness, own = 1.0, jax.random.fold_in(stream_key, 6)
    for dim, blocks in cuts:
        steps = jnp.exp(jax.random.uniform(jax.random.fold_in(own, dim), (blocks,), jnp.float32, smallest / len(cuts), largest / len(cuts)))
        loudness = loudness * jnp.repeat(steps, dims[dim] // blocks).reshape([-1 if axis == dim else 1 for axis in range(len(dims))])
    return loudness


def normal_values(rng, extent, deviation, most, cuts=(), held_as=jnp.bfloat16):
    result = deviation * jax.random.normal(rng, extent, jnp.float32)
    if cuts:
        result = result * block_levels(rng, extent, cuts, -0.22, 0.18)
    return jnp.clip(result, -most, most).astype(held_as)


def setup_inputs(seed: int = 0) -> dict:
    arg_keys = jax.random.split(jax.random.key(seed), 5)
    return {
        "b_tensor": draw_b_tensor(jax.random.fold_in(arg_keys[4], 71), 0),
        "density": normal_values(arg_keys[1], (NBAS, NBAS), NBAS ** -0.5, 0.25, ((0, 8),)),
        "pair_mask": draw_pair_mask(jax.random.fold_in(arg_keys[4], 71), 0),
        "dens_mask": draw_dens_mask(jax.random.fold_in(arg_keys[4], 71), 0),
    }


def expand(mask):
    return jnp.repeat(jnp.repeat(mask, BLK, axis=0), BLK, axis=1).astype(jnp.bfloat16)


def reference(b_tensor, density, pair_mask, dens_mask):
    pair_full = expand(pair_mask)
    dens_kept = density * expand(dens_mask)

    def accumulate(total, slab):
        kept = slab * pair_full
        half_x = jnp.dot(kept, dens_kept, preferred_element_type=jnp.float32).astype(jnp.bfloat16)
        return total + jnp.dot(half_x, kept.T, preferred_element_type=jnp.float32), None

    start = jnp.zeros((NBAS, NBAS), jnp.float32)
    total, unused = lax.scan(accumulate, start, b_tensor)
    return total
```

```python
import jax
import jax.numpy as jnp
from jax import lax
from jax.experimental import pallas as pl
from jax.experimental.pallas import tpu as pltpu
from jax.sharding import PartitionSpec as P

BF = jnp.bfloat16
F32 = jnp.float32
BLK = 64
TILE = 2 * BLK
CHIPS = 4
NEXT = {1: 2, 2: 3, 3: 1}


def expand_row(mask_ref, row, size):
    block = lax.broadcasted_iota(jnp.int32, (1, size), 1) // BLK
    line = jnp.zeros((1, size), F32)
    for j in range(size // BLK):
        line = jnp.where(block == j, mask_ref[row, j].astype(F32), line)
    return line.astype(BF)


def pack_kernel(group, b_ref, d_ref, pair_ref, dens_ref, own_ref, *send_refs):
    me = lax.axis_index("mu")
    c = me // 2
    size = b_ref.shape[2]
    pair_line = expand_row(pair_ref, me, size)
    dens = d_ref[...] * expand_row(dens_ref, me, size)
    for p in range(group):
        own_ref[p] = b_ref[c * group + p] * pair_line
    own_ref[group] = dens
    for d in (1, 2, 3):
        send = send_refs[d - 1]
        r = c ^ d
        n = c ^ d ^ NEXT[d]
        for slot, chip in enumerate((c, n)):
            cols = pl.ds(pl.multiple_of(chip * TILE, TILE), TILE)
            block = lax.broadcasted_iota(jnp.int32, (1, TILE), 1) // BLK
            line = jnp.where(block == 0, pair_ref[me, 2 * chip], pair_ref[me, 2 * chip + 1]).astype(F32).astype(BF)
            for p in range(group):
                send[p, :, slot * TILE : (slot + 1) * TILE] = b_ref[r * group + p, :, cols] * line
        half = size // 2
        send[group] = dens[:, :half]
        send[group + 1] = dens[:, half:]


def main_kernel(group, own_ref, mate_ref, r1, r2, r3, q1, q2, q3, e1, e2, e3, keep_ref, t_scr, d_scr, l_scr, x_scr, k_scr):
    me = lax.axis_index("mu")
    c = me // 2
    k = me % 2
    size = t_scr.shape[1]
    half = size // 2

    def rows(chip, core):
        return pl.multiple_of(chip * TILE + core * BLK, BLK)

    def cols(chip):
        return pl.ds(pl.multiple_of(chip * TILE, TILE), TILE)

    for core, own in ((k, own_ref), (1 - k, mate_ref)):
        d_scr[pl.ds(rows(c, core), BLK), :] = own[group]
        for p in range(group):
            t_scr[pl.ds(p * size + rows(c, core), BLK), :] = own[p]
    for d, mine, other in ((1, r1, q1), (2, r2, q2), (3, r3, q3)):
        r = c ^ d
        n = c ^ NEXT[d]
        for core, ref in ((k, mine), (1 - k, other)):
            d_scr[pl.ds(rows(r, core), BLK), :half] = ref[group]
            d_scr[pl.ds(rows(r, core), BLK), half:] = ref[group + 1]
            for p in range(group):
                at = pl.ds(p * size + rows(r, core), BLK)
                t_scr[at, cols(r)] = ref[p, :, :TILE]
                t_scr[at, cols(n)] = ref[p, :, TILE:]
    for d in (1, 2, 3):
        r = c ^ d
        n = c ^ NEXT[d]
        for p in range(group):
            for src, dst in ((c, r), (r, n)):
                block = t_scr[pl.ds(pl.multiple_of(p * size + src * TILE, TILE), TILE), cols(dst)]
                t_scr[pl.ds(pl.multiple_of(p * size + dst * TILE, TILE), TILE), cols(src)] = block.T
    for p in range(group):
        for r in range(CHIPS):
            l_scr[(p * CHIPS + r) * BLK : (p * CHIPS + r + 1) * BLK, :] = t_scr[pl.ds(p * size + rows(r, k), BLK), :]
    for p in range(group):
        x_scr[:, p * size : (p + 1) * size] = jnp.dot(
            l_scr[p * CHIPS * BLK : (p + 1) * CHIPS * BLK, :], d_scr[...], preferred_element_type=F32
        ).astype(BF)
    k_scr[...] = jnp.dot(x_scr[...], t_scr[...], preferred_element_type=F32)
    for d, out in ((1, e1), (2, e2), (3, e3)):
        out[...] = k_scr[pl.ds(pl.multiple_of((c ^ d) * BLK, BLK), BLK), :].astype(BF)
    keep_ref[...] = k_scr[pl.ds(pl.multiple_of(c * BLK, BLK), BLK), :]


def spread(b_tensor, density, pair_mask, dens_mask):
    depth, width, size = b_tensor.shape
    group = depth // CHIPS
    vmem = pl.BlockSpec(memory_space=pltpu.VMEM)
    smem = pl.BlockSpec(memory_space=pltpu.SMEM)

    def swap(x, step):
        return lax.ppermute(x, "mu", [(i, i ^ step) for i in range(2 * CHIPS)])

    piece = jax.ShapeDtypeStruct((group + 2, width, size // 2), BF)
    own, *sends = pl.pallas_call(
        lambda *refs: pack_kernel(group, *refs),
        out_shape=[jax.ShapeDtypeStruct((group + 1, width, size), BF), piece, piece, piece],
        in_specs=[vmem, vmem, smem, smem],
        out_specs=[vmem] * 4,
        compiler_params=pltpu.CompilerParams(vmem_limit_bytes=16 << 20),
        name="pack",
    )(b_tensor, density, pair_mask, dens_mask)
    got = [swap(send, 2 * d) for d, send in zip((1, 2, 3), sends)]
    mate = swap(own, 1)
    others = [swap(g, 1) for g in got]
    chunk = jax.ShapeDtypeStruct((width, size), BF)
    *parts, keep = pl.pallas_call(
        lambda *refs: main_kernel(group, *refs),
        out_shape=[chunk, chunk, chunk, jax.ShapeDtypeStruct((width, size), F32)],
        in_specs=[vmem] * 8,
        out_specs=[vmem] * 4,
        scratch_shapes=[
            pltpu.VMEM((group * size, size), BF),
            pltpu.VMEM((size, size), BF),
            pltpu.VMEM((group * size // 2, size), BF),
            pltpu.VMEM((size // 2, group * size), BF),
            pltpu.VMEM((size // 2, size), F32),
        ],
        compiler_params=pltpu.CompilerParams(vmem_limit_bytes=32 << 20),
        name="exchange",
    )(own, mate, *got, *others)
    plane = keep
    for d, part in zip((1, 2, 3), parts):
        plane = plane + swap(part, 2 * d).astype(F32)
    a = lax.axis_index("aux")
    strip = width // 4

    def strip_of(index):
        return lax.dynamic_slice_in_dim(plane, index * strip, strip, 0)

    total = strip_of(a)
    for d in (1, 2, 3):
        total = total + lax.ppermute(strip_of(a ^ d), "aux", [(i, i ^ d) for i in range(4)])
    return total


def gathered(b_tensor, density, pair_mask, dens_mask):
    depth, width, nbas = b_tensor.shape
    owner = lax.axis_index("mu")
    pair_row = lax.dynamic_slice_in_dim(pair_mask, owner, 1, 0)[0]
    dens_row = lax.dynamic_slice_in_dim(dens_mask, owner, 1, 0)[0]
    kept = b_tensor * jnp.repeat(pair_row, width).astype(BF)[None, None, :]
    dens_kept = density * jnp.repeat(dens_row, width).astype(BF)[None, :]
    summed = jnp.dot(
        kept.reshape(depth * width, nbas),
        lax.all_gather(dens_kept, "mu", axis=0, tiled=True),
        preferred_element_type=F32,
    )
    half_x = summed.astype(BF).reshape(depth, width, nbas)
    x_cols = lax.all_to_all(half_x, "mu", split_axis=2, concat_axis=1, tiled=True)
    partner = lax.all_to_all(kept, "mu", split_axis=2, concat_axis=1, tiled=True)
    return lax.psum_scatter(
        jnp.einsum("pms,pns->mn", x_cols, partner, preferred_element_type=F32),
        ("mu", "aux"),
        scatter_dimension=0,
        tiled=True,
    )


def solution(mesh):
    in_specs = (P("aux", "mu", None), P("mu", None), P(), P())
    out_specs = P(("mu", "aux"), None)

    def per_device(b_tensor, density, pair_mask, dens_mask):
        depth, width, size = b_tensor.shape
        fits = mesh.shape["mu"] == 2 * CHIPS and mesh.shape["aux"] == 4
        fits = fits and depth % CHIPS == 0 and width == BLK and size == 2 * CHIPS * BLK
        step = spread if fits else gathered
        return step(b_tensor, density, pair_mask, dens_mask)

    return jax.shard_map(per_device, mesh=mesh, in_specs=in_specs, out_specs=out_specs, check_vma=False)
```

```python
import jax
import jax.numpy as jnp
from jax import lax
from jax.experimental import pallas as pl
from jax.experimental.pallas import tpu as pltpu
from jax.sharding import PartitionSpec as P

BF = jnp.bfloat16
F32 = jnp.float32
BLK = 64
TILE = 2 * BLK
CHIPS = 4


def expand_row(mask_ref, row, size):
    block = lax.broadcasted_iota(jnp.int32, (1, size), 1) // BLK
    line = jnp.zeros((1, size), F32)
    for j in range(size // BLK):
        line = jnp.where(block == j, mask_ref[row, j].astype(F32), line)
    return line.astype(BF)


def column(chip):
    return pl.ds(pl.multiple_of(chip * TILE, TILE), TILE)


def pack_kernel(group, b_hbm, d_hbm, pair_hbm, dens_hbm, own_ref, s1, s2, s3, pair_ref, dens_ref, d_ref, line_ref, sems):
    me = lax.axis_index("mu")
    c = me // 2
    k = me % 2
    size = d_ref.shape[1]
    part = group // 2
    copies = [
        pltpu.make_async_copy(pair_hbm, pair_ref, sems.at[0]),
        pltpu.make_async_copy(dens_hbm, dens_ref, sems.at[1]),
        pltpu.make_async_copy(d_hbm, d_ref, sems.at[2]),
    ]
    pieces = []
    for send, d in ((s1, 1 + k), (s2, 2 - k), (s3, 3)):
        first = (c ^ d) * group
        pieces.append((send, 0, group, first, c))
        if send is not s3:
            pieces.append((send, group, group, first, c ^ (3 - d)))
            pieces.append((send, 2 * group, part, first + (d - 1) * part, c ^ 3))
    for i, (send, slot, count, first, chip) in enumerate(pieces):
        copies.append(
            pltpu.make_async_copy(
                b_hbm.at[pl.ds(first, count), :, column(chip)], send.at[pl.ds(slot, count)], sems.at[3 + i]
            )
        )
    copies.append(
        pltpu.make_async_copy(b_hbm.at[pl.ds(c * group, group)], own_ref.at[pl.ds(0, group)], sems.at[3 + len(pieces)])
    )
    for copy in copies:
        copy.start()
    copies[0].wait()
    pair_line = expand_row(pair_ref, me, size)
    for j in range(CHIPS):
        line_ref[j] = pair_line[:, j * TILE : (j + 1) * TILE].astype(F32)
    copies[1].wait()
    dens_line = expand_row(dens_ref, me, size)
    copies[2].wait()
    dens = d_ref[...] * dens_line
    own_dens = [dens[:, (2 * (j % CHIPS) + j // CHIPS) * BLK :][:, :BLK] for j in range(2 * CHIPS)]
    tiles = [jnp.concatenate(own_dens[2 * j : 2 * j + 2], axis=1) for j in range(CHIPS)]
    for j in range(CHIPS):
        own_ref[group, :, j * TILE : (j + 1) * TILE] = tiles[j]
        for send in (s1, s2, s3):
            send[send.shape[0] - CHIPS + j] = tiles[j]
    for copy, (send, slot, count, first, chip) in zip(copies[3:], pieces):
        copy.wait()
        line = line_ref[chip].astype(BF)
        for p in range(slot, slot + count):
            send[p] = send[p] * line
    copies[-1].wait()
    for p in range(group):
        own_ref[p] = own_ref[p] * pair_line


def main_kernel(group, own_ref, mate_ref, r1, r2, r3, q1, q2, q3, e1, e2, e3, keep_ref, t_scr, d_scr, x_scr, k_scr):
    me = lax.axis_index("mu")
    c = me // 2
    k = me % 2
    size = t_scr.shape[1]
    half = size // 2
    part = group // 2

    def rows(p, core, chip):
        return pl.ds(pl.multiple_of(p * size + core * half + chip * BLK, BLK), BLK)

    def fill(o0, o1, x0, y0, g0, x1, y1, g1):
        cx, cy, cg = c ^ 1, c ^ 2, c ^ 3
        for core, own, x, y, g in ((0, o0, x0, y0, g0), (1, o1, x1, y1, g1)):
            d_scr[pl.ds(pl.multiple_of(c * TILE + core * BLK, BLK), BLK), :] = own[group]
            for r, ref in ((cx, x), (cy, y), (cg, g)):
                at = pl.ds(pl.multiple_of(r * TILE + core * BLK, BLK), BLK)
                for j in range(CHIPS):
                    d_scr[at, j * TILE : (j + 1) * TILE] = ref[ref.shape[0] - CHIPS + j]
            for p in range(group):
                t_scr[rows(p, core, c), :] = own[p]
                t_scr[rows(p, core, cx), column(cx)] = x[p]
                t_scr[rows(p, core, cx), column(cg)] = x[group + p]
                t_scr[rows(p, core, cy), column(cy)] = y[p]
                t_scr[rows(p, core, cy), column(cg)] = y[group + p]
                t_scr[rows(p, core, cg), column(cg)] = g[p]
                if p < part:
                    t_scr[rows(p, core, cx), column(cy)] = x[2 * group + p]
                else:
                    t_scr[rows(p, core, cy), column(cx)] = y[2 * group + p - part]
        for p in range(group):
            tasks = [(c, dst, o0[p, :, column(dst)], o1[p, :, column(dst)]) for dst in (cx, cy, cg)]
            tasks.append((cx, cg, x0[group + p], x1[group + p]))
            tasks.append((cy, cg, y0[group + p], y1[group + p]))
            if p < part:
                tasks.append((cx, cy, x0[2 * group + p], x1[2 * group + p]))
            else:
                tasks.append((cy, cx, y0[2 * group + p - part], y1[2 * group + p - part]))
            for s, dst, top, low in tasks:
                block = jnp.concatenate([top, low], axis=0).T
                t_scr[rows(p, 0, dst), column(s)] = block[:BLK]
                t_scr[rows(p, 1, dst), column(s)] = block[BLK:]

    @pl.when(k == 0)
    def _():
        fill(own_ref, mate_ref, r1, r2, r3, q2, q1, q3)

    @pl.when(k == 1)
    def _():
        fill(mate_ref, own_ref, q1, q2, q3, r2, r1, r3)

    for p in range(group):
        mine = t_scr[pl.ds(pl.multiple_of(p * size + k * half, half), half), :]
        x_scr[:, p * size : (p + 1) * size] = jnp.dot(mine, d_scr[...], preferred_element_type=F32).astype(BF)
    k_scr[...] = jnp.dot(x_scr[...], t_scr[...], preferred_element_type=F32)
    for out, d in ((e1, 1 + k), (e2, 2 - k), (e3, 3)):
        out[...] = k_scr[pl.ds(pl.multiple_of((c ^ d) * BLK, BLK), BLK), :].astype(BF)
    keep_ref[...] = k_scr[pl.ds(pl.multiple_of(c * BLK, BLK), BLK), :]


def spread(b_tensor, density, pair_mask, dens_mask):
    depth, width, size = b_tensor.shape
    group = depth // CHIPS
    vmem = pl.BlockSpec(memory_space=pltpu.VMEM)
    hbm = pl.BlockSpec(memory_space=pl.ANY)

    def swap(x, step):
        return lax.ppermute(x, "mu", [(i, i ^ step) for i in range(2 * CHIPS)])

    def turn(x, first):
        return lax.ppermute(x, "mu", [(i, i ^ (2 if (i % 2 == 0) == first else 4)) for i in range(2 * CHIPS)])

    def around(x1, x2, x3):
        return turn(x1, True), turn(x2, False), swap(x3, 6)

    def slots(count):
        return jax.ShapeDtypeStruct((count, width, TILE), BF)

    near = 2 * group + group // 2 + CHIPS
    own, *sends = pl.pallas_call(
        lambda *refs: pack_kernel(group, *refs),
        out_shape=[jax.ShapeDtypeStruct((group + 1, width, size), BF), slots(near), slots(near), slots(group + CHIPS)],
        in_specs=[hbm] * 4,
        out_specs=[vmem] * 4,
        scratch_shapes=[
            pltpu.SMEM(pair_mask.shape, jnp.int32),
            pltpu.SMEM(dens_mask.shape, jnp.int32),
            pltpu.VMEM(density.shape, BF),
            pltpu.VMEM((CHIPS, 1, TILE), F32),
            pltpu.SemaphoreType.DMA((11,)),
        ],
        compiler_params=pltpu.CompilerParams(vmem_limit_bytes=16 << 20),
        name="pack",
    )(*(pltpu.with_memory_space_constraint(x, pltpu.HBM) for x in (b_tensor, density, pair_mask, dens_mask)))
    got = around(*sends)
    mate = swap(own, 1)
    others = [swap(g, 1) for g in got]
    chunk = jax.ShapeDtypeStruct((width, size), BF)
    *parts, keep = pl.pallas_call(
        lambda *refs: main_kernel(group, *refs),
        out_shape=[chunk, chunk, chunk, jax.ShapeDtypeStruct((width, size), F32)],
        in_specs=[vmem] * 8,
        out_specs=[vmem] * 4,
        scratch_shapes=[
            pltpu.VMEM((group * size, size), BF),
            pltpu.VMEM((size, size), BF),
            pltpu.VMEM((size // 2, group * size), BF),
            pltpu.VMEM((size // 2, size), F32),
        ],
        compiler_params=pltpu.CompilerParams(vmem_limit_bytes=32 << 20),
        name="exchange",
    )(own, mate, *got, *others)
    plane = keep
    for part in around(*parts):
        plane = plane + part.astype(F32)
    a = lax.axis_index("aux")
    strips = plane.reshape(2, 2, width // 4, size)

    def pick(x, index, axis):
        return lax.dynamic_index_in_dim(x, index, axis, keepdims=False)

    def along(x, step):
        return lax.ppermute(x, "aux", [(i, i ^ step) for i in range(4)])

    pair = pick(strips, a % 2, 1) + along(pick(strips, 1 - a % 2, 1), 1)
    return pick(pair, a // 2, 0) + along(pick(pair, 1 - a // 2, 0), 2)


def gathered(b_tensor, density, pair_mask, dens_mask):
    depth, width, nbas = b_tensor.shape
    owner = lax.axis_index("mu")
    pair_row = lax.dynamic_slice_in_dim(pair_mask, owner, 1, 0)[0]
    dens_row = lax.dynamic_slice_in_dim(dens_mask, owner, 1, 0)[0]
    kept = b_tensor * jnp.repeat(pair_row, width).astype(BF)[None, None, :]
    dens_kept = density * jnp.repeat(dens_row, width).astype(BF)[None, :]
    summed = jnp.dot(
        kept.reshape(depth * width, nbas),
        lax.all_gather(dens_kept, "mu", axis=0, tiled=True),
        preferred_element_type=F32,
    )
    half_x = summed.astype(BF).reshape(depth, width, nbas)
    x_cols = lax.all_to_all(half_x, "mu", split_axis=2, concat_axis=1, tiled=True)
    partner = lax.all_to_all(kept, "mu", split_axis=2, concat_axis=1, tiled=True)
    return lax.psum_scatter(
        jnp.einsum("pms,pns->mn", x_cols, partner, preferred_element_type=F32),
        ("mu", "aux"),
        scatter_dimension=0,
        tiled=True,
    )


def solution(mesh):
    in_specs = (P("aux", "mu", None), P("mu", None), P(), P())
    out_specs = P(("mu", "aux"), None)

    def per_device(b_tensor, density, pair_mask, dens_mask):
        depth, width, size = b_tensor.shape
        fits = mesh.shape["mu"] == 2 * CHIPS and mesh.shape["aux"] == 4
        fits = fits and depth % CHIPS == 0 and width == BLK and size == 2 * CHIPS * BLK
        step = spread if fits else gathered
        return step(b_tensor, density, pair_mask, dens_mask)

    return jax.shard_map(per_device, mesh=mesh, in_specs=in_specs, out_specs=out_specs, check_vma=False)
```

```python
import jax
import jax.numpy as jnp
from jax import lax
from jax.experimental import pallas as pl
from jax.experimental.pallas import tpu as pltpu
from jax.sharding import PartitionSpec as P

BF = jnp.bfloat16
F32 = jnp.float32
BLK = 64
TILE = 2 * BLK
CHIPS = 4
GROUP = 4
NEAR = 13
FAR = 7


def expand_row(mask_ref, row, size):
    block = lax.broadcasted_iota(jnp.int32, (1, size), 1) // BLK
    line = jnp.zeros((1, size), F32)
    for j in range(size // BLK):
        line = jnp.where(block == j, mask_ref[row, j].astype(F32), line)
    return line.astype(BF)


def column(chip):
    return pl.ds(pl.multiple_of(chip * TILE, TILE), TILE)


def pack_kernel(
    b_hbm, d_hbm, pair_hbm, dens_hbm, own_ref, s1, s2, s3, pair_ref, dens_ref, d_ref, half_ref, line_ref, sems
):
    me = lax.axis_index("mu")
    c = me // 2
    k = me % 2
    size = d_ref.shape[1]
    copies = [
        pltpu.make_async_copy(pair_hbm, pair_ref, sems.at[0]),
        pltpu.make_async_copy(dens_hbm, dens_ref, sems.at[1]),
        pltpu.make_async_copy(d_hbm, d_ref, sems.at[2]),
    ]
    pieces = []
    for i, (send, d) in enumerate(((s1, 1 + k), (s2, 2 - k), (s3, 3))):
        first = (c ^ d) * GROUP
        pieces.append((send, 0, 2, first + 2 * k, c))
        pieces.append((half_ref, 2 * i, 2, first + 2 * (1 - k), c))
        if send is not s3:
            pieces.append((send, 3, GROUP, first, c ^ (3 - d)))
            pieces.append((send, 7, 2, first + 2 * (d - 1), c ^ 3))
    for i, (into, slot, count, first, chip) in enumerate(pieces):
        copies.append(
            pltpu.make_async_copy(
                b_hbm.at[pl.ds(first, count), :, column(chip)], into.at[pl.ds(slot, count)], sems.at[3 + i]
            )
        )
    copies.append(
        pltpu.make_async_copy(b_hbm.at[pl.ds(c * GROUP, GROUP)], own_ref.at[pl.ds(0, GROUP)], sems.at[3 + len(pieces)])
    )
    for copy in copies:
        copy.start()
    copies[0].wait()
    pair_line = expand_row(pair_ref, me, size)
    for j in range(CHIPS):
        line_ref[j] = pair_line[:, j * TILE : (j + 1) * TILE].astype(F32)
    copies[1].wait()
    dens_line = expand_row(dens_ref, me, size)
    copies[2].wait()
    dens = d_ref[...] * dens_line
    own_ref[GROUP] = dens
    for j in range(CHIPS):
        for send in (s1, s2, s3):
            send[send.shape[0] - CHIPS + j] = dens[:, j * TILE : (j + 1) * TILE]
    for copy, (into, slot, count, first, chip) in zip(copies[3:], pieces):
        copy.wait()
        line = line_ref[chip].astype(BF)
        for p in range(slot, slot + count):
            into[p] = into[p] * line
    for core in (0, 1):

        @pl.when(k == core)
        def _():
            for i, send in enumerate((s1, s2, s3)):
                left, right = (half_ref[2 * i + j][:, core * BLK : (core + 1) * BLK] for j in (0, 1))
                send[2] = jnp.concatenate([left, right], axis=1)

    copies[-1].wait()
    for p in range(GROUP):
        own_ref[p] = own_ref[p] * pair_line


def row_at(p, chip, core):
    return pl.ds(pl.multiple_of(p * 2 * CHIPS * BLK + chip * TILE + core * BLK, BLK), BLK)


def square(p, b0, b1):
    if p < 2:
        corner = b0[p].T[BLK:]
        return b0[p], jnp.concatenate([corner, b1[2][:, p * BLK : (p + 1) * BLK]], axis=1)
    corner = b1[p - 2].T[:BLK]
    return jnp.concatenate([b0[2][:, (p - 2) * BLK : (p - 1) * BLK], corner], axis=1), b1[p - 2]


def early_kernel(own_ref, mate_ref, r1, r2, q1, q2, t_ref, l_ref, x_ref, d_scr, l_scr):
    me = lax.axis_index("mu")
    c = me // 2
    k = me % 2
    size = t_ref.shape[1]
    cx, cy, cg = c ^ 1, c ^ 2, c ^ 3

    def fill(o0, o1, x0, y0, x1, y1):
        for core, own, x, y in ((0, o0, x0, y0), (1, o1, x1, y1)):
            d_scr[row_at(0, c, core), :] = own[GROUP]
            for r, ref in ((cx, x), (cy, y)):
                for j in range(CHIPS):
                    d_scr[row_at(0, r, core), j * TILE : (j + 1) * TILE] = ref[NEAR - CHIPS + j]
            d_scr[row_at(0, cg, core), :] = jnp.zeros((BLK, size), BF)
            for p in range(GROUP):
                t_ref[row_at(p, c, core), :] = own[p]
                t_ref[row_at(p, cx, core), column(cg)] = x[3 + p]
                t_ref[row_at(p, cy, core), column(cg)] = y[3 + p]
                t_ref[row_at(p, cg, core), column(cg)] = jnp.zeros((BLK, TILE), BF)
                if p < 2:
                    t_ref[row_at(p, cx, core), column(cy)] = x[7 + p]
                else:
                    t_ref[row_at(p, cy, core), column(cx)] = y[5 + p]
        for p in range(GROUP):
            for r, b0, b1 in ((cx, x0, x1), (cy, y0, y1)):
                top, low = square(p, b0, b1)
                t_ref[row_at(p, r, 0), column(r)] = top
                t_ref[row_at(p, r, 1), column(r)] = low
            tasks = [(c, dst, o0[p, :, column(dst)], o1[p, :, column(dst)]) for dst in (cx, cy, cg)]
            tasks.append((cx, cg, x0[3 + p], x1[3 + p]))
            tasks.append((cy, cg, y0[3 + p], y1[3 + p]))
            if p < 2:
                tasks.append((cx, cy, x0[7 + p], x1[7 + p]))
            else:
                tasks.append((cy, cx, y0[5 + p], y1[5 + p]))
            for src, dst, top, low in tasks:
                block = jnp.concatenate([top, low], axis=0).T
                t_ref[row_at(p, dst, 0), column(src)] = block[:BLK]
                t_ref[row_at(p, dst, 1), column(src)] = block[BLK:]

    @pl.when(k == 0)
    def _():
        fill(own_ref, mate_ref, r1, r2, q2, q1)

    @pl.when(k == 1)
    def _():
        fill(mate_ref, own_ref, q1, q2, r2, r1)

    for p in range(GROUP):
        for r in range(CHIPS):
            at = slice((p * CHIPS + r) * BLK, (p * CHIPS + r + 1) * BLK)
            l_scr[at, :] = t_ref[row_at(p, r, k), :]
            l_ref[at, :] = t_ref[row_at(p, r, k), column(cg)]
    x_ref[...] = jnp.dot(l_scr[...], d_scr[...], preferred_element_type=F32)


def late_kernel(t_ref, l_ref, xp_ref, r3, q3, e1, e2, e3, keep_ref, d_scr, l_scr, g_scr, x_scr, xg_scr, k_scr):
    me = lax.axis_index("mu")
    c = me // 2
    k = me % 2
    size = t_ref.shape[1]
    half = size // 2
    cg = c ^ 3

    def fill(g0, g1):
        for core, g in ((0, g0), (1, g1)):
            for j in range(CHIPS):
                d_scr[core * BLK : (core + 1) * BLK, j * TILE : (j + 1) * TILE] = g[FAR - CHIPS + j]
        for p in range(GROUP):
            top, low = square(p, g0, g1)
            g_scr[p * TILE : p * TILE + BLK, :] = top
            g_scr[p * TILE + BLK : (p + 1) * TILE, :] = low

    @pl.when(k == 0)
    def _():
        fill(r3, q3)

    @pl.when(k == 1)
    def _():
        fill(q3, r3)

    l_scr[...] = l_ref[...]
    for p in range(GROUP):
        at = pl.ds(pl.multiple_of((p * CHIPS + cg) * BLK, BLK), BLK)
        l_scr[at, :] = g_scr[pl.ds(pl.multiple_of(p * TILE + k * BLK, BLK), BLK), :]
    for p in range(GROUP):
        rest = jnp.dot(l_scr[p * half : (p + 1) * half, :], d_scr[...], preferred_element_type=F32)
        x_scr[:, p * size : (p + 1) * size] = (xp_ref[p * half : (p + 1) * half, :] + rest).astype(BF)
        xg_scr[:, p * TILE : (p + 1) * TILE] = x_scr[:, pl.ds(pl.multiple_of(p * size + cg * TILE, TILE), TILE)]
    k_scr[...] = jnp.dot(x_scr[...], t_ref[...], preferred_element_type=F32)
    k_scr[:, column(cg)] += jnp.dot(xg_scr[...], g_scr[...], preferred_element_type=F32)
    for out, d in ((e1, 1 + k), (e2, 2 - k), (e3, 3)):
        out[...] = k_scr[pl.ds(pl.multiple_of((c ^ d) * BLK, BLK), BLK), :].astype(BF)
    keep_ref[...] = k_scr[pl.ds(pl.multiple_of(c * BLK, BLK), BLK), :]


def spread(b_tensor, density, pair_mask, dens_mask):
    width, size = density.shape
    vmem = pl.BlockSpec(memory_space=pltpu.VMEM)
    hbm = pl.BlockSpec(memory_space=pl.ANY)

    def swap(x, step):
        return lax.ppermute(x, "mu", [(i, i ^ step) for i in range(2 * CHIPS)])

    def turn(x, first):
        return lax.ppermute(x, "mu", [(i, i ^ (2 if (i % 2 == 0) == first else 4)) for i in range(2 * CHIPS)])

    def around(x1, x2, x3):
        return turn(x1, True), turn(x2, False), swap(x3, 6)

    def slots(count):
        return jax.ShapeDtypeStruct((count, width, TILE), BF)

    own, *sends = pl.pallas_call(
        pack_kernel,
        out_shape=[jax.ShapeDtypeStruct((GROUP + 1, width, size), BF), slots(NEAR), slots(NEAR), slots(FAR)],
        in_specs=[hbm] * 4,
        out_specs=[vmem] * 4,
        scratch_shapes=[
            pltpu.SMEM(pair_mask.shape, jnp.int32),
            pltpu.SMEM(dens_mask.shape, jnp.int32),
            pltpu.VMEM(density.shape, BF),
            pltpu.VMEM((6, width, TILE), BF),
            pltpu.VMEM((CHIPS, 1, TILE), F32),
            pltpu.SemaphoreType.DMA((14,)),
        ],
        compiler_params=pltpu.CompilerParams(vmem_limit_bytes=16 << 20),
        name="pack",
    )(*(pltpu.with_memory_space_constraint(x, pltpu.HBM) for x in (b_tensor, density, pair_mask, dens_mask)))
    r1, r2, r3 = around(*sends)
    mate = swap(own, 1)
    q1, q2, q3 = swap(r1, 1), swap(r2, 1), swap(r3, 1)
    half = size // 2
    early = pl.pallas_call(
        early_kernel,
        out_shape=[
            jax.ShapeDtypeStruct((GROUP * size, size), BF),
            jax.ShapeDtypeStruct((GROUP * half, TILE), BF),
            jax.ShapeDtypeStruct((GROUP * half, size), F32),
        ],
        in_specs=[vmem] * 6,
        out_specs=[vmem] * 3,
        scratch_shapes=[pltpu.VMEM((size, size), BF), pltpu.VMEM((GROUP * half, size), BF)],
        compiler_params=pltpu.CompilerParams(vmem_limit_bytes=32 << 20),
        name="early",
    )(own, mate, r1, r2, q1, q2)
    chunk = jax.ShapeDtypeStruct((width, size), BF)
    *parts, keep = pl.pallas_call(
        late_kernel,
        out_shape=[chunk, chunk, chunk, jax.ShapeDtypeStruct((width, size), F32)],
        in_specs=[vmem] * 5,
        out_specs=[vmem] * 4,
        scratch_shapes=[
            pltpu.VMEM((TILE, size), BF),
            pltpu.VMEM((GROUP * half, TILE), BF),
            pltpu.VMEM((GROUP * TILE, TILE), BF),
            pltpu.VMEM((half, GROUP * size), BF),
            pltpu.VMEM((half, GROUP * TILE), BF),
            pltpu.VMEM((half, size), F32),
        ],
        compiler_params=pltpu.CompilerParams(vmem_limit_bytes=32 << 20),
        name="late",
    )(*early, r3, q3)
    y1, y2, y3 = around(*parts)
    plane = (((keep + y3.astype(F32)) + y1.astype(F32)) + y2.astype(F32))
    a = lax.axis_index("aux")
    strip = width // 4

    def strip_of(index):
        return lax.dynamic_slice_in_dim(plane, index * strip, strip, 0)

    def along(step):
        return lax.ppermute(strip_of(a ^ step), "aux", [(i, i ^ step) for i in range(4)])

    z1, z2, z3 = along(1), along(2), along(3)
    return ((strip_of(a) + z2) + z3) + z1


def gathered(b_tensor, density, pair_mask, dens_mask):
    depth, width, nbas = b_tensor.shape
    owner = lax.axis_index("mu")
    pair_row = lax.dynamic_slice_in_dim(pair_mask, owner, 1, 0)[0]
    dens_row = lax.dynamic_slice_in_dim(dens_mask, owner, 1, 0)[0]
    kept = b_tensor * jnp.repeat(pair_row, width).astype(BF)[None, None, :]
    dens_kept = density * jnp.repeat(dens_row, width).astype(BF)[None, :]
    summed = jnp.dot(
        kept.reshape(depth * width, nbas),
        lax.all_gather(dens_kept, "mu", axis=0, tiled=True),
        preferred_element_type=F32,
    )
    half_x = summed.astype(BF).reshape(depth, width, nbas)
    x_cols = lax.all_to_all(half_x, "mu", split_axis=2, concat_axis=1, tiled=True)
    partner = lax.all_to_all(kept, "mu", split_axis=2, concat_axis=1, tiled=True)
    return lax.psum_scatter(
        jnp.einsum("pms,pns->mn", x_cols, partner, preferred_element_type=F32),
        ("mu", "aux"),
        scatter_dimension=0,
        tiled=True,
    )


def solution(mesh):
    in_specs = (P("aux", "mu", None), P("mu", None), P(), P())
    out_specs = P(("mu", "aux"), None)

    def per_device(b_tensor, density, pair_mask, dens_mask):
        depth, width, size = b_tensor.shape
        fits = mesh.shape["mu"] == 2 * CHIPS and mesh.shape["aux"] == 4
        fits = fits and depth == GROUP * CHIPS and width == BLK and size == 2 * CHIPS * BLK
        step = spread if fits else gathered
        return step(b_tensor, density, pair_mask, dens_mask)

    return jax.shard_map(per_device, mesh=mesh, in_specs=in_specs, out_specs=out_specs, check_vma=False)
```

```python
import jax
import jax.numpy as jnp
from jax import lax
from jax.experimental import pallas as pl
from jax.experimental.pallas import tpu as pltpu
from jax.sharding import PartitionSpec as P

BF = jnp.bfloat16
F32 = jnp.float32
BLK = 64
TILE = 2 * BLK
CHIPS = 4
GROUP = 4
STEPS = ((2, 3, 1, 0), (3, 2, 0, 1), (1, 0, 3, 2))
NEAR = 13
FAR = 7


def expand_row(mask_ref, row, size):
    block = lax.broadcasted_iota(jnp.int32, (1, size), 1) // BLK
    line = jnp.zeros((1, size), F32)
    for j in range(size // BLK):
        line = jnp.where(block == j, mask_ref[row, j].astype(F32), line)
    return line.astype(BF)


def column(chip):
    return pl.ds(pl.multiple_of(chip * TILE, TILE), TILE)


def pack_kernel(
    b_hbm, d_hbm, pair_hbm, dens_hbm, own_ref, s1, s2, s3, pair_ref, dens_ref, d_ref, half_ref, line_ref, sems
):
    me = lax.axis_index("mu")
    c = me // 2
    k = me % 2
    size = d_ref.shape[1]
    copies = [
        pltpu.make_async_copy(pair_hbm, pair_ref, sems.at[0]),
        pltpu.make_async_copy(dens_hbm, dens_ref, sems.at[1]),
        pltpu.make_async_copy(d_hbm, d_ref, sems.at[2]),
    ]
    pieces = []
    for i, (send, d) in enumerate(((s1, 1 + k), (s2, 2 - k), (s3, 3))):
        first = (c ^ d) * GROUP
        pieces.append((send, 0, 2, first + 2 * k, c))
        pieces.append((half_ref, 2 * i, 2, first + 2 * (1 - k), c))
        if send is not s3:
            pieces.append((send, 3, GROUP, first, c ^ (3 - d)))
            pieces.append((send, 7, 2, first + 2 * (d - 1), c ^ 3))
    for i, (into, slot, count, first, chip) in enumerate(pieces):
        copies.append(
            pltpu.make_async_copy(
                b_hbm.at[pl.ds(first, count), :, column(chip)], into.at[pl.ds(slot, count)], sems.at[3 + i]
            )
        )
    copies.append(
        pltpu.make_async_copy(b_hbm.at[pl.ds(c * GROUP, GROUP)], own_ref.at[pl.ds(0, GROUP)], sems.at[3 + len(pieces)])
    )
    for copy in copies:
        copy.start()
    copies[0].wait()
    pair_line = expand_row(pair_ref, me, size)
    for j in range(CHIPS):
        line_ref[j] = pair_line[:, j * TILE : (j + 1) * TILE].astype(F32)
    copies[1].wait()
    dens_line = expand_row(dens_ref, me, size)
    copies[2].wait()
    dens = d_ref[...] * dens_line
    own_ref[GROUP] = dens
    for j in range(CHIPS):
        for send in (s1, s2, s3):
            send[send.shape[0] - CHIPS + j] = dens[:, j * TILE : (j + 1) * TILE]
    for copy, (into, slot, count, first, chip) in zip(copies[3:], pieces):
        copy.wait()
        line = line_ref[chip].astype(BF)
        for p in range(slot, slot + count):
            into[p] = into[p] * line
    for core in (0, 1):

        @pl.when(k == core)
        def _():
            for i, send in enumerate((s1, s2, s3)):
                left, right = (half_ref[2 * i + j][:, core * BLK : (core + 1) * BLK] for j in (0, 1))
                send[2] = jnp.concatenate([left, right], axis=1)

    copies[-1].wait()
    for p in range(GROUP):
        own_ref[p] = own_ref[p] * pair_line


def row_at(p, chip, core):
    return pl.ds(pl.multiple_of(p * 2 * CHIPS * BLK + chip * TILE + core * BLK, BLK), BLK)


def square(p, b0, b1):
    if p < 2:
        corner = b0[p].T[BLK:]
        return b0[p], jnp.concatenate([corner, b1[2][:, p * BLK : (p + 1) * BLK]], axis=1)
    corner = b1[p - 2].T[:BLK]
    return jnp.concatenate([b0[2][:, (p - 2) * BLK : (p - 1) * BLK], corner], axis=1), b1[p - 2]


def early_kernel(own_ref, mate_ref, r1, r2, q1, q2, t_ref, l_ref, x_ref, d_scr, l_scr):
    me = lax.axis_index("mu")
    c = me // 2
    k = me % 2
    size = t_ref.shape[1]
    cx, cy, cg = c ^ 1, c ^ 2, c ^ 3

    def fill(o0, o1, x0, y0, x1, y1):
        for core, own, x, y in ((0, o0, x0, y0), (1, o1, x1, y1)):
            d_scr[row_at(0, c, core), :] = own[GROUP]
            for r, ref in ((cx, x), (cy, y)):
                for j in range(CHIPS):
                    d_scr[row_at(0, r, core), j * TILE : (j + 1) * TILE] = ref[NEAR - CHIPS + j]
            d_scr[row_at(0, cg, core), :] = jnp.zeros((BLK, size), BF)
            for p in range(GROUP):
                t_ref[row_at(p, c, core), :] = own[p]
                t_ref[row_at(p, cx, core), column(cg)] = x[3 + p]
                t_ref[row_at(p, cy, core), column(cg)] = y[3 + p]
                t_ref[row_at(p, cg, core), column(cg)] = jnp.zeros((BLK, TILE), BF)
                if p < 2:
                    t_ref[row_at(p, cx, core), column(cy)] = x[7 + p]
                else:
                    t_ref[row_at(p, cy, core), column(cx)] = y[5 + p]
        for p in range(GROUP):
            for r, b0, b1 in ((cx, x0, x1), (cy, y0, y1)):
                top, low = square(p, b0, b1)
                t_ref[row_at(p, r, 0), column(r)] = top
                t_ref[row_at(p, r, 1), column(r)] = low
            tasks = [(c, dst, o0[p, :, column(dst)], o1[p, :, column(dst)]) for dst in (cx, cy, cg)]
            tasks.append((cx, cg, x0[3 + p], x1[3 + p]))
            tasks.append((cy, cg, y0[3 + p], y1[3 + p]))
            if p < 2:
                tasks.append((cx, cy, x0[7 + p], x1[7 + p]))
            else:
                tasks.append((cy, cx, y0[5 + p], y1[5 + p]))
            for src, dst, top, low in tasks:
                block = jnp.concatenate([top, low], axis=0).T
                t_ref[row_at(p, dst, 0), column(src)] = block[:BLK]
                t_ref[row_at(p, dst, 1), column(src)] = block[BLK:]

    @pl.when(k == 0)
    def _():
        fill(own_ref, mate_ref, r1, r2, q2, q1)

    @pl.when(k == 1)
    def _():
        fill(mate_ref, own_ref, q1, q2, r2, r1)

    for p in range(GROUP):
        for r in range(CHIPS):
            at = slice((p * CHIPS + r) * BLK, (p * CHIPS + r + 1) * BLK)
            l_scr[at, :] = t_ref[row_at(p, r, k), :]
            l_ref[at, :] = t_ref[row_at(p, r, k), column(cg)]
    x_ref[...] = jnp.dot(l_scr[...], d_scr[...], preferred_element_type=F32)


def late_kernel(t_ref, l_ref, xp_ref, r3, q3, e1, e2, e3, keep_ref, d_scr, l_scr, g_scr, x_scr, xg_scr, k_scr):
    me = lax.axis_index("mu")
    c = me // 2
    k = me % 2
    size = t_ref.shape[1]
    half = size // 2
    cg = c ^ 3

    def fill(g0, g1):
        for core, g in ((0, g0), (1, g1)):
            for j in range(CHIPS):
                d_scr[core * BLK : (core + 1) * BLK, j * TILE : (j + 1) * TILE] = g[FAR - CHIPS + j]
        for p in range(GROUP):
            top, low = square(p, g0, g1)
            g_scr[p * TILE : p * TILE + BLK, :] = top
            g_scr[p * TILE + BLK : (p + 1) * TILE, :] = low

    @pl.when(k == 0)
    def _():
        fill(r3, q3)

    @pl.when(k == 1)
    def _():
        fill(q3, r3)

    l_scr[...] = l_ref[...]
    for p in range(GROUP):
        at = pl.ds(pl.multiple_of((p * CHIPS + cg) * BLK, BLK), BLK)
        l_scr[at, :] = g_scr[pl.ds(pl.multiple_of(p * TILE + k * BLK, BLK), BLK), :]
    for p in range(GROUP):
        rest = jnp.dot(l_scr[p * half : (p + 1) * half, :], d_scr[...], preferred_element_type=F32)
        x_scr[:, p * size : (p + 1) * size] = (xp_ref[p * half : (p + 1) * half, :] + rest).astype(BF)
        xg_scr[:, p * TILE : (p + 1) * TILE] = x_scr[:, pl.ds(pl.multiple_of(p * size + cg * TILE, TILE), TILE)]
    k_scr[...] = jnp.dot(x_scr[...], t_ref[...], preferred_element_type=F32)
    k_scr[:, column(cg)] += jnp.dot(xg_scr[...], g_scr[...], preferred_element_type=F32)
    for out, d in ((e1, 1 + k), (e2, 2 - k), (e3, 3)):
        out[...] = k_scr[pl.ds(pl.multiple_of((c ^ d) * BLK, BLK), BLK), :].astype(BF)
    keep_ref[...] = k_scr[pl.ds(pl.multiple_of(c * BLK, BLK), BLK), :]


def spread(b_tensor, density, pair_mask, dens_mask):
    width, size = density.shape
    vmem = pl.BlockSpec(memory_space=pltpu.VMEM)
    hbm = pl.BlockSpec(memory_space=pl.ANY)

    def swap(x, step):
        return lax.ppermute(x, "mu", [(i, i ^ step) for i in range(2 * CHIPS)])

    def turn(x, first):
        return lax.ppermute(x, "mu", [(i, i ^ (2 if (i % 2 == 0) == first else 4)) for i in range(2 * CHIPS)])

    def around(x1, x2, x3):
        return turn(x1, True), turn(x2, False), swap(x3, 6)

    def slots(count):
        return jax.ShapeDtypeStruct((count, width, TILE), BF)

    own, *sends = pl.pallas_call(
        pack_kernel,
        out_shape=[jax.ShapeDtypeStruct((GROUP + 1, width, size), BF), slots(NEAR), slots(NEAR), slots(FAR)],
        in_specs=[hbm] * 4,
        out_specs=[vmem] * 4,
        scratch_shapes=[
            pltpu.SMEM(pair_mask.shape, jnp.int32),
            pltpu.SMEM(dens_mask.shape, jnp.int32),
            pltpu.VMEM(density.shape, BF),
            pltpu.VMEM((6, width, TILE), BF),
            pltpu.VMEM((CHIPS, 1, TILE), F32),
            pltpu.SemaphoreType.DMA((14,)),
        ],
        compiler_params=pltpu.CompilerParams(vmem_limit_bytes=16 << 20),
        name="pack",
    )(*(pltpu.with_memory_space_constraint(x, pltpu.HBM) for x in (b_tensor, density, pair_mask, dens_mask)))
    r1, r2, r3 = around(*sends)
    mate = swap(own, 1)
    q1, q2, q3 = swap(r1, 1), swap(r2, 1), swap(r3, 1)
    half = size // 2
    early = pl.pallas_call(
        early_kernel,
        out_shape=[
            jax.ShapeDtypeStruct((GROUP * size, size), BF),
            jax.ShapeDtypeStruct((GROUP * half, TILE), BF),
            jax.ShapeDtypeStruct((GROUP * half, size), F32),
        ],
        in_specs=[vmem] * 6,
        out_specs=[vmem] * 3,
        scratch_shapes=[pltpu.VMEM((size, size), BF), pltpu.VMEM((GROUP * half, size), BF)],
        compiler_params=pltpu.CompilerParams(vmem_limit_bytes=32 << 20),
        name="early",
    )(own, mate, r1, r2, q1, q2)
    chunk = jax.ShapeDtypeStruct((width, size), BF)
    *parts, keep = pl.pallas_call(
        late_kernel,
        out_shape=[chunk, chunk, chunk, jax.ShapeDtypeStruct((width, size), F32)],
        in_specs=[vmem] * 5,
        out_specs=[vmem] * 4,
        scratch_shapes=[
            pltpu.VMEM((TILE, size), BF),
            pltpu.VMEM((GROUP * half, TILE), BF),
            pltpu.VMEM((GROUP * TILE, TILE), BF),
            pltpu.VMEM((half, GROUP * size), BF),
            pltpu.VMEM((half, GROUP * TILE), BF),
            pltpu.VMEM((half, size), F32),
        ],
        compiler_params=pltpu.CompilerParams(vmem_limit_bytes=32 << 20),
        name="late",
    )(*early, r3, q3)
    y1, y2, y3 = around(*parts)
    plane = (((keep + y3.astype(F32)) + y1.astype(F32)) + y2.astype(F32))
    a = lax.axis_index("aux")
    strip = width // 4

    def strip_of(index):
        return lax.dynamic_slice_in_dim(plane, index * strip, strip, 0)

    total = strip_of(a)
    for step in STEPS:
        to = sum(jnp.where(a == i, j, 0) for i, j in enumerate(step))
        total = total + lax.ppermute(strip_of(to), "aux", list(enumerate(step)))
    return total


def gathered(b_tensor, density, pair_mask, dens_mask):
    depth, width, nbas = b_tensor.shape
    owner = lax.axis_index("mu")
    pair_row = lax.dynamic_slice_in_dim(pair_mask, owner, 1, 0)[0]
    dens_row = lax.dynamic_slice_in_dim(dens_mask, owner, 1, 0)[0]
    kept = b_tensor * jnp.repeat(pair_row, width).astype(BF)[None, None, :]
    dens_kept = density * jnp.repeat(dens_row, width).astype(BF)[None, :]
    summed = jnp.dot(
        kept.reshape(depth * width, nbas),
        lax.all_gather(dens_kept, "mu", axis=0, tiled=True),
        preferred_element_type=F32,
    )
    half_x = summed.astype(BF).reshape(depth, width, nbas)
    x_cols = lax.all_to_all(half_x, "mu", split_axis=2, concat_axis=1, tiled=True)
    partner = lax.all_to_all(kept, "mu", split_axis=2, concat_axis=1, tiled=True)
    return lax.psum_scatter(
        jnp.einsum("pms,pns->mn", x_cols, partner, preferred_element_type=F32),
        ("mu", "aux"),
        scatter_dimension=0,
        tiled=True,
    )


def solution(mesh):
    in_specs = (P("aux", "mu", None), P("mu", None), P(), P())
    out_specs = P(("mu", "aux"), None)

    def per_device(b_tensor, density, pair_mask, dens_mask):
        depth, width, size = b_tensor.shape
        fits = mesh.shape["mu"] == 2 * CHIPS and mesh.shape["aux"] == 4
        fits = fits and depth == GROUP * CHIPS and width == BLK and size == 2 * CHIPS * BLK
        step = spread if fits else gathered
        return step(b_tensor, density, pair_mask, dens_mask)

    return jax.shard_map(per_device, mesh=mesh, in_specs=in_specs, out_specs=out_specs, check_vma=False)
```

```python
import jax
import jax.numpy as jnp
from jax import lax
from jax.experimental import pallas as pl
from jax.experimental.pallas import tpu as pltpu
from jax.sharding import PartitionSpec as P

BF = jnp.bfloat16
F32 = jnp.float32
BLK = 64
TILE = 2 * BLK
CHIPS = 4
GROUP = 4
PLANE = ((1, 3, 0, 2), (3, 2, 1, 0), (2, 0, 3, 1))
STEPS = ((2, 3, 1, 0), (3, 2, 0, 1), (1, 0, 3, 2))
NEAR = 13
FAR = 7


def expand_row(mask_ref, row, size):
    block = lax.broadcasted_iota(jnp.int32, (1, size), 1) // BLK
    line = jnp.zeros((1, size), F32)
    for j in range(size // BLK):
        line = jnp.where(block == j, mask_ref[row, j].astype(F32), line)
    return line.astype(BF)


def column(chip):
    return pl.ds(pl.multiple_of(chip * TILE, TILE), TILE)


def pack_kernel(
    b_hbm, d_hbm, pair_hbm, dens_hbm, s1, s2, s3, mine_ref, line_ref, pair_ref, dens_ref, d_ref, half_ref, sems
):
    me = lax.axis_index("mu")
    c = me // 2
    k = me % 2
    size = d_ref.shape[1]
    copies = [
        pltpu.make_async_copy(pair_hbm, pair_ref, sems.at[0]),
        pltpu.make_async_copy(dens_hbm, dens_ref, sems.at[1]),
        pltpu.make_async_copy(d_hbm, d_ref, sems.at[2]),
    ]
    pieces = []
    for i, (send, d) in enumerate(((s1, 1 + k), (s2, 2 - k), (s3, 3))):
        first = (c ^ d) * GROUP
        pieces.append((send, 0, 2, first + 2 * k, c))
        pieces.append((half_ref, 2 * i, 2, first + 2 * (1 - k), c))
        if send is not s3:
            pieces.append((send, 3, GROUP, first, c ^ (3 - d)))
            pieces.append((send, 7, 2, first + 2 * (d - 1), c ^ 3))
    for i, (into, slot, count, first, chip) in enumerate(pieces):
        copies.append(
            pltpu.make_async_copy(
                b_hbm.at[pl.ds(first, count), :, column(chip)], into.at[pl.ds(slot, count)], sems.at[3 + i]
            )
        )
    for copy in copies:
        copy.start()
    copies[0].wait()
    pair_line = expand_row(pair_ref, me, size)
    for j in range(CHIPS):
        line_ref[j] = pair_line[:, j * TILE : (j + 1) * TILE].astype(F32)
    copies[1].wait()
    dens_line = expand_row(dens_ref, me, size)
    copies[2].wait()
    dens = d_ref[...] * dens_line
    mine_ref[...] = dens
    for j in range(CHIPS):
        for send in (s1, s2, s3):
            send[send.shape[0] - CHIPS + j] = dens[:, j * TILE : (j + 1) * TILE]
    for copy, (into, slot, count, first, chip) in zip(copies[3:], pieces):
        copy.wait()
        line = line_ref[chip].astype(BF)
        for p in range(slot, slot + count):
            into[p] = into[p] * line
    for core in (0, 1):

        @pl.when(k == core)
        def _():
            for i, send in enumerate((s1, s2, s3)):
                left, right = (half_ref[2 * i + j][:, core * BLK : (core + 1) * BLK] for j in (0, 1))
                send[2] = jnp.concatenate([left, right], axis=1)


def own_kernel(b_hbm, mine_ref, line_ref, own_ref, sem):
    c = lax.axis_index("mu") // 2
    copy = pltpu.make_async_copy(b_hbm.at[pl.ds(c * GROUP, GROUP)], own_ref.at[pl.ds(0, GROUP)], sem)
    copy.start()
    own_ref[GROUP] = mine_ref[...]
    copy.wait()
    for p in range(GROUP):
        for j in range(CHIPS):
            at = slice(j * TILE, (j + 1) * TILE)
            own_ref[p, :, at] = own_ref[p, :, at] * line_ref[j].astype(BF)


def row_at(p, chip, core):
    return pl.ds(pl.multiple_of(p * 2 * CHIPS * BLK + chip * TILE + core * BLK, BLK), BLK)


def square(p, b0, b1):
    if p < 2:
        corner = b0[p].T[BLK:]
        return b0[p], jnp.concatenate([corner, b1[2][:, p * BLK : (p + 1) * BLK]], axis=1)
    corner = b1[p - 2].T[:BLK]
    return jnp.concatenate([b0[2][:, (p - 2) * BLK : (p - 1) * BLK], corner], axis=1), b1[p - 2]


def early_kernel(own_ref, mate_ref, r1, r2, q1, q2, t_ref, l_ref, x_ref, d_scr, l_scr):
    me = lax.axis_index("mu")
    c = me // 2
    k = me % 2
    size = t_ref.shape[1]
    cx, cy, cg = c ^ 1, c ^ 2, c ^ 3

    def fill(o0, o1, x0, y0, x1, y1):
        for core, own, x, y in ((0, o0, x0, y0), (1, o1, x1, y1)):
            d_scr[row_at(0, c, core), :] = own[GROUP]
            for r, ref in ((cx, x), (cy, y)):
                for j in range(CHIPS):
                    d_scr[row_at(0, r, core), j * TILE : (j + 1) * TILE] = ref[NEAR - CHIPS + j]
            d_scr[row_at(0, cg, core), :] = jnp.zeros((BLK, size), BF)
            for p in range(GROUP):
                t_ref[row_at(p, c, core), :] = own[p]
                t_ref[row_at(p, cx, core), column(cg)] = x[3 + p]
                t_ref[row_at(p, cy, core), column(cg)] = y[3 + p]
                t_ref[row_at(p, cg, core), column(cg)] = jnp.zeros((BLK, TILE), BF)
                if p < 2:
                    t_ref[row_at(p, cx, core), column(cy)] = x[7 + p]
                else:
                    t_ref[row_at(p, cy, core), column(cx)] = y[5 + p]
        for p in range(GROUP):
            for r, b0, b1 in ((cx, x0, x1), (cy, y0, y1)):
                top, low = square(p, b0, b1)
                t_ref[row_at(p, r, 0), column(r)] = top
                t_ref[row_at(p, r, 1), column(r)] = low
            tasks = [(c, dst, o0[p, :, column(dst)], o1[p, :, column(dst)]) for dst in (cx, cy, cg)]
            tasks.append((cx, cg, x0[3 + p], x1[3 + p]))
            tasks.append((cy, cg, y0[3 + p], y1[3 + p]))
            if p < 2:
                tasks.append((cx, cy, x0[7 + p], x1[7 + p]))
            else:
                tasks.append((cy, cx, y0[5 + p], y1[5 + p]))
            for src, dst, top, low in tasks:
                block = jnp.concatenate([top, low], axis=0).T
                t_ref[row_at(p, dst, 0), column(src)] = block[:BLK]
                t_ref[row_at(p, dst, 1), column(src)] = block[BLK:]

    @pl.when(k == 0)
    def _():
        fill(own_ref, mate_ref, r1, r2, q2, q1)

    @pl.when(k == 1)
    def _():
        fill(mate_ref, own_ref, q1, q2, r2, r1)

    for p in range(GROUP):
        for r in range(CHIPS):
            at = slice((p * CHIPS + r) * BLK, (p * CHIPS + r + 1) * BLK)
            l_scr[at, :] = t_ref[row_at(p, r, k), :]
            l_ref[at, :] = t_ref[row_at(p, r, k), column(cg)]
    x_ref[...] = jnp.dot(l_scr[...], d_scr[...], preferred_element_type=F32)


def late_kernel(t_ref, l_ref, xp_ref, r3, q3, e1, e2, e3, keep_ref, d_scr, l_scr, g_scr, x_scr, xg_scr, k_scr):
    me = lax.axis_index("mu")
    c = me // 2
    k = me % 2
    size = t_ref.shape[1]
    half = size // 2
    cg = c ^ 3

    def fill(g0, g1):
        for core, g in ((0, g0), (1, g1)):
            for j in range(CHIPS):
                d_scr[core * BLK : (core + 1) * BLK, j * TILE : (j + 1) * TILE] = g[FAR - CHIPS + j]
        for p in range(GROUP):
            top, low = square(p, g0, g1)
            g_scr[p * TILE : p * TILE + BLK, :] = top
            g_scr[p * TILE + BLK : (p + 1) * TILE, :] = low

    @pl.when(k == 0)
    def _():
        fill(r3, q3)

    @pl.when(k == 1)
    def _():
        fill(q3, r3)

    l_scr[...] = l_ref[...]
    for p in range(GROUP):
        at = pl.ds(pl.multiple_of((p * CHIPS + cg) * BLK, BLK), BLK)
        l_scr[at, :] = g_scr[pl.ds(pl.multiple_of(p * TILE + k * BLK, BLK), BLK), :]
    for p in range(GROUP):
        rest = jnp.dot(l_scr[p * half : (p + 1) * half, :], d_scr[...], preferred_element_type=F32)
        x_scr[:, p * size : (p + 1) * size] = (xp_ref[p * half : (p + 1) * half, :] + rest).astype(BF)
        xg_scr[:, p * TILE : (p + 1) * TILE] = x_scr[:, pl.ds(pl.multiple_of(p * size + cg * TILE, TILE), TILE)]
    k_scr[...] = jnp.dot(x_scr[...], t_ref[...], preferred_element_type=F32)
    k_scr[:, column(cg)] += jnp.dot(xg_scr[...], g_scr[...], preferred_element_type=F32)
    for out, step in zip((e1, e2, e3), PLANE):
        to = sum(jnp.where(c == i, j, 0) for i, j in enumerate(step))
        out[...] = k_scr[pl.ds(pl.multiple_of(to * BLK, BLK), BLK), :].astype(BF)
    keep_ref[...] = k_scr[pl.ds(pl.multiple_of(c * BLK, BLK), BLK), :]


def spread(b_tensor, density, pair_mask, dens_mask):
    width, size = density.shape
    vmem = pl.BlockSpec(memory_space=pltpu.VMEM)
    hbm = pl.BlockSpec(memory_space=pl.ANY)

    def swap(x, step):
        return lax.ppermute(x, "mu", [(i, i ^ step) for i in range(2 * CHIPS)])

    def turn(x, first):
        return lax.ppermute(x, "mu", [(i, i ^ (2 if (i % 2 == 0) == first else 4)) for i in range(2 * CHIPS)])

    def around(x1, x2, x3):
        return turn(x1, True), turn(x2, False), swap(x3, 6)

    def slots(count):
        return jax.ShapeDtypeStruct((count, width, TILE), BF)

    b_tensor, density, pair_mask, dens_mask = (
        pltpu.with_memory_space_constraint(x, pltpu.HBM) for x in (b_tensor, density, pair_mask, dens_mask)
    )
    *sends, mine, line = pl.pallas_call(
        pack_kernel,
        out_shape=[
            slots(NEAR),
            slots(NEAR),
            slots(FAR),
            jax.ShapeDtypeStruct((width, size), BF),
            jax.ShapeDtypeStruct((CHIPS, 1, TILE), F32),
        ],
        in_specs=[hbm] * 4,
        out_specs=[vmem] * 5,
        scratch_shapes=[
            pltpu.SMEM(pair_mask.shape, jnp.int32),
            pltpu.SMEM(dens_mask.shape, jnp.int32),
            pltpu.VMEM(density.shape, BF),
            pltpu.VMEM((6, width, TILE), BF),
            pltpu.SemaphoreType.DMA((13,)),
        ],
        compiler_params=pltpu.CompilerParams(vmem_limit_bytes=16 << 20),
        name="pack",
    )(b_tensor, density, pair_mask, dens_mask)
    own = pl.pallas_call(
        own_kernel,
        out_shape=jax.ShapeDtypeStruct((GROUP + 1, width, size), BF),
        in_specs=[hbm, vmem, vmem],
        out_specs=vmem,
        scratch_shapes=[pltpu.SemaphoreType.DMA],
        compiler_params=pltpu.CompilerParams(vmem_limit_bytes=16 << 20),
        name="own",
    )(b_tensor, mine, line)
    r1, r2, r3 = around(*sends)
    mate = swap(own, 1)
    q1, q2, q3 = swap(r1, 1), swap(r2, 1), swap(r3, 1)
    half = size // 2
    early = pl.pallas_call(
        early_kernel,
        out_shape=[
            jax.ShapeDtypeStruct((GROUP * size, size), BF),
            jax.ShapeDtypeStruct((GROUP * half, TILE), BF),
            jax.ShapeDtypeStruct((GROUP * half, size), F32),
        ],
        in_specs=[vmem] * 6,
        out_specs=[vmem] * 3,
        scratch_shapes=[pltpu.VMEM((size, size), BF), pltpu.VMEM((GROUP * half, size), BF)],
        compiler_params=pltpu.CompilerParams(vmem_limit_bytes=32 << 20),
        name="early",
    )(own, mate, r1, r2, q1, q2)
    chunk = jax.ShapeDtypeStruct((width, size), BF)
    *parts, keep = pl.pallas_call(
        late_kernel,
        out_shape=[chunk, chunk, chunk, jax.ShapeDtypeStruct((width, size), F32)],
        in_specs=[vmem] * 5,
        out_specs=[vmem] * 4,
        scratch_shapes=[
            pltpu.VMEM((TILE, size), BF),
            pltpu.VMEM((GROUP * half, TILE), BF),
            pltpu.VMEM((GROUP * TILE, TILE), BF),
            pltpu.VMEM((half, GROUP * size), BF),
            pltpu.VMEM((half, GROUP * TILE), BF),
            pltpu.VMEM((half, size), F32),
        ],
        compiler_params=pltpu.CompilerParams(vmem_limit_bytes=32 << 20),
        name="late",
    )(*early, r3, q3)
    plane = keep
    for part, step in zip(parts, PLANE):
        pairs = [(2 * i + core, 2 * j + core) for i, j in enumerate(step) for core in (0, 1)]
        plane = plane + lax.ppermute(part, "mu", pairs).astype(F32)
    a = lax.axis_index("aux")
    strip = width // 4

    def strip_of(index):
        return lax.dynamic_slice_in_dim(plane, index * strip, strip, 0)

    total = strip_of(a)
    for step in STEPS:
        to = sum(jnp.where(a == i, j, 0) for i, j in enumerate(step))
        total = total + lax.ppermute(strip_of(to), "aux", list(enumerate(step)))
    return total


def gathered(b_tensor, density, pair_mask, dens_mask):
    depth, width, nbas = b_tensor.shape
    owner = lax.axis_index("mu")
    pair_row = lax.dynamic_slice_in_dim(pair_mask, owner, 1, 0)[0]
    dens_row = lax.dynamic_slice_in_dim(dens_mask, owner, 1, 0)[0]
    kept = b_tensor * jnp.repeat(pair_row, width).astype(BF)[None, None, :]
    dens_kept = density * jnp.repeat(dens_row, width).astype(BF)[None, :]
    summed = jnp.dot(
        kept.reshape(depth * width, nbas),
        lax.all_gather(dens_kept, "mu", axis=0, tiled=True),
        preferred_element_type=F32,
    )
    half_x = summed.astype(BF).reshape(depth, width, nbas)
    x_cols = lax.all_to_all(half_x, "mu", split_axis=2, concat_axis=1, tiled=True)
    partner = lax.all_to_all(kept, "mu", split_axis=2, concat_axis=1, tiled=True)
    return lax.psum_scatter(
        jnp.einsum("pms,pns->mn", x_cols, partner, preferred_element_type=F32),
        ("mu", "aux"),
        scatter_dimension=0,
        tiled=True,
    )


def solution(mesh):
    in_specs = (P("aux", "mu", None), P("mu", None), P(), P())
    out_specs = P(("mu", "aux"), None)

    def per_device(b_tensor, density, pair_mask, dens_mask):
        depth, width, size = b_tensor.shape
        fits = mesh.shape["mu"] == 2 * CHIPS and mesh.shape["aux"] == 4
        fits = fits and depth == GROUP * CHIPS and width == BLK and size == 2 * CHIPS * BLK
        step = spread if fits else gathered
        return step(b_tensor, density, pair_mask, dens_mask)

    return jax.shard_map(per_device, mesh=mesh, in_specs=in_specs, out_specs=out_specs, check_vma=False)
```

```python
import jax
import jax.numpy as jnp
from jax import lax
from jax.experimental import pallas as pl
from jax.experimental.pallas import tpu as pltpu
from jax.sharding import PartitionSpec as P

BF = jnp.bfloat16
F32 = jnp.float32
BLK = 64
TILE = 2 * BLK
CHIPS = 4
GROUP = 4
STEPS = ((2, 3, 1, 0), (3, 2, 0, 1), (1, 0, 3, 2))
NEAR = 13
FAR = 7


def expand_row(mask_ref, row, size):
    block = lax.broadcasted_iota(jnp.int32, (1, size), 1) // BLK
    line = jnp.zeros((1, size), F32)
    for j in range(size // BLK):
        line = jnp.where(block == j, mask_ref[row, j].astype(F32), line)
    return line.astype(BF)


def column(chip):
    return pl.ds(pl.multiple_of(chip * TILE, TILE), TILE)


def pack_kernel(
    b_hbm, d_hbm, pair_hbm, dens_hbm, own_ref, s1, s2, s3, pair_ref, dens_ref, d_ref, half_ref, line_ref, sems
):
    me = lax.axis_index("mu")
    c = me // 2
    k = me % 2
    size = d_ref.shape[1]
    copies = [
        pltpu.make_async_copy(pair_hbm, pair_ref, sems.at[0]),
        pltpu.make_async_copy(dens_hbm, dens_ref, sems.at[1]),
        pltpu.make_async_copy(d_hbm, d_ref, sems.at[2]),
    ]
    pieces = []
    for i, (send, d) in enumerate(((s1, 1 + k), (s2, 2 - k), (s3, 3))):
        first = (c ^ d) * GROUP
        pieces.append((send, 0, 2, first + 2 * k, c))
        pieces.append((half_ref, 2 * i, 2, first + 2 * (1 - k), c))
        if send is not s3:
            pieces.append((send, 3, GROUP, first, c ^ (3 - d)))
            pieces.append((send, 7, 2, first + 2 * (d - 1), c ^ 3))
    for i, (into, slot, count, first, chip) in enumerate(pieces):
        copies.append(
            pltpu.make_async_copy(
                b_hbm.at[pl.ds(first, count), :, column(chip)], into.at[pl.ds(slot, count)], sems.at[3 + i]
            )
        )
    copies.append(
        pltpu.make_async_copy(b_hbm.at[pl.ds(c * GROUP, GROUP)], own_ref.at[pl.ds(0, GROUP)], sems.at[3 + len(pieces)])
    )
    for copy in copies:
        copy.start()
    copies[0].wait()
    pair_line = expand_row(pair_ref, me, size)
    for j in range(CHIPS):
        line_ref[j] = pair_line[:, j * TILE : (j + 1) * TILE].astype(F32)
    copies[1].wait()
    dens_line = expand_row(dens_ref, me, size)
    copies[2].wait()
    dens = d_ref[...] * dens_line
    own_ref[GROUP] = dens
    for j in range(CHIPS):
        for send in (s1, s2, s3):
            send[send.shape[0] - CHIPS + j] = dens[:, j * TILE : (j + 1) * TILE]
    for copy, (into, slot, count, first, chip) in zip(copies[3:], pieces):
        copy.wait()
        line = line_ref[chip].astype(BF)
        for p in range(slot, slot + count):
            into[p] = into[p] * line
    for core in (0, 1):

        @pl.when(k == core)
        def _():
            for i, send in enumerate((s1, s2, s3)):
                left, right = (half_ref[2 * i + j][:, core * BLK : (core + 1) * BLK] for j in (0, 1))
                send[2] = jnp.concatenate([left, right], axis=1)

    copies[-1].wait()
    for p in range(GROUP):
        own_ref[p] = own_ref[p] * pair_line


def row_at(p, chip, core):
    return pl.ds(pl.multiple_of(p * 2 * CHIPS * BLK + chip * TILE + core * BLK, BLK), BLK)


def square(p, b0, b1):
    if p < 2:
        corner = b0[p].T[BLK:]
        return b0[p], jnp.concatenate([corner, b1[2][:, p * BLK : (p + 1) * BLK]], axis=1)
    corner = b1[p - 2].T[:BLK]
    return jnp.concatenate([b0[2][:, (p - 2) * BLK : (p - 1) * BLK], corner], axis=1), b1[p - 2]


def early_kernel(own_ref, mate_ref, r1, r2, q1, q2, t_ref, l_ref, x_ref, d_scr, l_scr):
    me = lax.axis_index("mu")
    c = me // 2
    k = me % 2
    size = t_ref.shape[1]
    cx, cy, cg = c ^ 1, c ^ 2, c ^ 3

    def fill(o0, o1, x0, y0, x1, y1):
        for core, own, x, y in ((0, o0, x0, y0), (1, o1, x1, y1)):
            d_scr[row_at(0, c, core), :] = own[GROUP]
            for r, ref in ((cx, x), (cy, y)):
                for j in range(CHIPS):
                    d_scr[row_at(0, r, core), j * TILE : (j + 1) * TILE] = ref[NEAR - CHIPS + j]
            d_scr[row_at(0, cg, core), :] = jnp.zeros((BLK, size), BF)
            for p in range(GROUP):
                t_ref[row_at(p, c, core), :] = own[p]
                t_ref[row_at(p, cx, core), column(cg)] = x[3 + p]
                t_ref[row_at(p, cy, core), column(cg)] = y[3 + p]
                t_ref[row_at(p, cg, core), column(cg)] = jnp.zeros((BLK, TILE), BF)
                if p < 2:
                    t_ref[row_at(p, cx, core), column(cy)] = x[7 + p]
                else:
                    t_ref[row_at(p, cy, core), column(cx)] = y[5 + p]
        for p in range(GROUP):
            for r, b0, b1 in ((cx, x0, x1), (cy, y0, y1)):
                top, low = square(p, b0, b1)
                t_ref[row_at(p, r, 0), column(r)] = top
                t_ref[row_at(p, r, 1), column(r)] = low
            tasks = [(c, dst, o0[p, :, column(dst)], o1[p, :, column(dst)]) for dst in (cx, cy, cg)]
            tasks.append((cx, cg, x0[3 + p], x1[3 + p]))
            tasks.append((cy, cg, y0[3 + p], y1[3 + p]))
            if p < 2:
                tasks.append((cx, cy, x0[7 + p], x1[7 + p]))
            else:
                tasks.append((cy, cx, y0[5 + p], y1[5 + p]))
            for src, dst, top, low in tasks:
                block = jnp.concatenate([top, low], axis=0).T
                t_ref[row_at(p, dst, 0), column(src)] = block[:BLK]
                t_ref[row_at(p, dst, 1), column(src)] = block[BLK:]

    @pl.when(k == 0)
    def _():
        fill(own_ref, mate_ref, r1, r2, q2, q1)

    @pl.when(k == 1)
    def _():
        fill(mate_ref, own_ref, q1, q2, r2, r1)

    for p in range(GROUP):
        for r in range(CHIPS):
            at = slice((p * CHIPS + r) * BLK, (p * CHIPS + r + 1) * BLK)
            l_scr[at, :] = t_ref[row_at(p, r, k), :]
            l_ref[at, :] = t_ref[row_at(p, r, k), column(cg)]
    x_ref[...] = jnp.dot(l_scr[...], d_scr[...], preferred_element_type=F32)


def late_kernel(t_in, l_ref, xp_ref, r3, q3, e1, e2, e3, keep_ref, t_ref, d_scr, l_scr, x_scr, k_scr):
    me = lax.axis_index("mu")
    c = me // 2
    k = me % 2
    size = t_ref.shape[1]
    half = size // 2
    cg = c ^ 3

    def fill(g0, g1):
        for core, g in ((0, g0), (1, g1)):
            for j in range(CHIPS):
                d_scr[core * BLK : (core + 1) * BLK, j * TILE : (j + 1) * TILE] = g[FAR - CHIPS + j]
        for p in range(GROUP):
            top, low = square(p, g0, g1)
            t_ref[row_at(p, cg, 0), column(cg)] = top
            t_ref[row_at(p, cg, 1), column(cg)] = low

    @pl.when(k == 0)
    def _():
        fill(r3, q3)

    @pl.when(k == 1)
    def _():
        fill(q3, r3)

    l_scr[...] = l_ref[...]
    for p in range(GROUP):
        at = pl.ds(pl.multiple_of((p * CHIPS + cg) * BLK, BLK), BLK)
        l_scr[at, :] = t_ref[row_at(p, cg, k), column(cg)]
    for p in range(GROUP):
        rest = jnp.dot(l_scr[p * half : (p + 1) * half, :], d_scr[...], preferred_element_type=F32)
        x_scr[:, p * size : (p + 1) * size] = (xp_ref[p * half : (p + 1) * half, :] + rest).astype(BF)
    k_scr[...] = jnp.dot(x_scr[...], t_ref[...], preferred_element_type=F32)
    for out, d in ((e1, 1 + k), (e2, 2 - k), (e3, 3)):
        out[...] = k_scr[pl.ds(pl.multiple_of((c ^ d) * BLK, BLK), BLK), :].astype(BF)
    keep_ref[...] = k_scr[pl.ds(pl.multiple_of(c * BLK, BLK), BLK), :]


def spread(b_tensor, density, pair_mask, dens_mask):
    width, size = density.shape
    vmem = pl.BlockSpec(memory_space=pltpu.VMEM)
    hbm = pl.BlockSpec(memory_space=pl.ANY)

    def swap(x, step):
        return lax.ppermute(x, "mu", [(i, i ^ step) for i in range(2 * CHIPS)])

    def turn(x, first):
        return lax.ppermute(x, "mu", [(i, i ^ (2 if (i % 2 == 0) == first else 4)) for i in range(2 * CHIPS)])

    def around(x1, x2, x3):
        return turn(x1, True), turn(x2, False), swap(x3, 6)

    def slots(count):
        return jax.ShapeDtypeStruct((count, width, TILE), BF)

    own, *sends = pl.pallas_call(
        pack_kernel,
        out_shape=[jax.ShapeDtypeStruct((GROUP + 1, width, size), BF), slots(NEAR), slots(NEAR), slots(FAR)],
        in_specs=[hbm] * 4,
        out_specs=[vmem] * 4,
        scratch_shapes=[
            pltpu.SMEM(pair_mask.shape, jnp.int32),
            pltpu.SMEM(dens_mask.shape, jnp.int32),
            pltpu.VMEM(density.shape, BF),
            pltpu.VMEM((6, width, TILE), BF),
            pltpu.VMEM((CHIPS, 1, TILE), F32),
            pltpu.SemaphoreType.DMA((14,)),
        ],
        compiler_params=pltpu.CompilerParams(vmem_limit_bytes=16 << 20),
        name="pack",
    )(*(pltpu.with_memory_space_constraint(x, pltpu.HBM) for x in (b_tensor, density, pair_mask, dens_mask)))
    r1, r2, r3 = around(*sends)
    mate = swap(own, 1)
    q1, q2, q3 = swap(r1, 1), swap(r2, 1), swap(r3, 1)
    half = size // 2
    early = pl.pallas_call(
        early_kernel,
        out_shape=[
            jax.ShapeDtypeStruct((GROUP * size, size), BF),
            jax.ShapeDtypeStruct((GROUP * half, TILE), BF),
            jax.ShapeDtypeStruct((GROUP * half, size), F32),
        ],
        in_specs=[vmem] * 6,
        out_specs=[vmem] * 3,
        scratch_shapes=[pltpu.VMEM((size, size), BF), pltpu.VMEM((GROUP * half, size), BF)],
        compiler_params=pltpu.CompilerParams(vmem_limit_bytes=32 << 20),
        name="early",
    )(own, mate, r1, r2, q1, q2)
    chunk = jax.ShapeDtypeStruct((width, size), BF)
    *parts, keep, unused = pl.pallas_call(
        late_kernel,
        out_shape=[chunk, chunk, chunk, jax.ShapeDtypeStruct((width, size), F32), jax.ShapeDtypeStruct(early[0].shape, BF)],
        in_specs=[vmem] * 5,
        out_specs=[vmem] * 5,
        input_output_aliases={0: 4},
        scratch_shapes=[
            pltpu.VMEM((TILE, size), BF),
            pltpu.VMEM((GROUP * half, TILE), BF),
            pltpu.VMEM((half, GROUP * size), BF),
            pltpu.VMEM((half, size), F32),
        ],
        compiler_params=pltpu.CompilerParams(vmem_limit_bytes=32 << 20),
        name="late",
    )(*early, r3, q3)
    y1, y2, y3 = around(*parts)
    plane = (((keep + y3.astype(F32)) + y1.astype(F32)) + y2.astype(F32))
    a = lax.axis_index("aux")
    strip = width // 4

    def strip_of(index):
        return lax.dynamic_slice_in_dim(plane, index * strip, strip, 0)

    total = strip_of(a)
    for step in STEPS:
        to = sum(jnp.where(a == i, j, 0) for i, j in enumerate(step))
        total = total + lax.ppermute(strip_of(to), "aux", list(enumerate(step)))
    return total


def gathered(b_tensor, density, pair_mask, dens_mask):
    depth, width, nbas = b_tensor.shape
    owner = lax.axis_index("mu")
    pair_row = lax.dynamic_slice_in_dim(pair_mask, owner, 1, 0)[0]
    dens_row = lax.dynamic_slice_in_dim(dens_mask, owner, 1, 0)[0]
    kept = b_tensor * jnp.repeat(pair_row, width).astype(BF)[None, None, :]
    dens_kept = density * jnp.repeat(dens_row, width).astype(BF)[None, :]
    summed = jnp.dot(
        kept.reshape(depth * width, nbas),
        lax.all_gather(dens_kept, "mu", axis=0, tiled=True),
        preferred_element_type=F32,
    )
    half_x = summed.astype(BF).reshape(depth, width, nbas)
    x_cols = lax.all_to_all(half_x, "mu", split_axis=2, concat_axis=1, tiled=True)
    partner = lax.all_to_all(kept, "mu", split_axis=2, concat_axis=1, tiled=True)
    return lax.psum_scatter(
        jnp.einsum("pms,pns->mn", x_cols, partner, preferred_element_type=F32),
        ("mu", "aux"),
        scatter_dimension=0,
        tiled=True,
    )


def solution(mesh):
    in_specs = (P("aux", "mu", None), P("mu", None), P(), P())
    out_specs = P(("mu", "aux"), None)

    def per_device(b_tensor, density, pair_mask, dens_mask):
        depth, width, size = b_tensor.shape
        fits = mesh.shape["mu"] == 2 * CHIPS and mesh.shape["aux"] == 4
        fits = fits and depth == GROUP * CHIPS and width == BLK and size == 2 * CHIPS * BLK
        step = spread if fits else gathered
        return step(b_tensor, density, pair_mask, dens_mask)

    return jax.shard_map(per_device, mesh=mesh, in_specs=in_specs, out_specs=out_specs, check_vma=False)
```

```python
import jax
import jax.numpy as jnp
from jax import lax
from jax.experimental import pallas as pl
from jax.experimental.pallas import tpu as pltpu
from jax.sharding import PartitionSpec as P

BF = jnp.bfloat16
F32 = jnp.float32
BLK = 64
TILE = 2 * BLK
CHIPS = 4
LAYERS = 4
STRIP = BLK // LAYERS
Z_FIRST = 1
ALONG_ONE = ((3, 2, 1, 0), (1, 0, 3, 2), (2, 3, 0, 1))
PLANE_TWO = ((3, 2, 1, 0), (1, 0, 3, 2), (2, 3, 0, 1))
PLANE_ONE = ((1, 3, 0, 2), (3, 2, 1, 0), (2, 0, 3, 1))
ALONG_TWO = ((2, 3, 1, 0), (3, 2, 0, 1), (1, 0, 3, 2))
GROUP = 4
NEAR = 13
FAR = 7


def expand_row(mask_ref, row, size):
    block = lax.broadcasted_iota(jnp.int32, (1, size), 1) // BLK
    line = jnp.zeros((1, size), F32)
    for j in range(size // BLK):
        line = jnp.where(block == j, mask_ref[row, j].astype(F32), line)
    return line.astype(BF)


def column(chip):
    return pl.ds(pl.multiple_of(chip * TILE, TILE), TILE)


def pack_kernel(
    b_hbm, d_hbm, pair_hbm, dens_hbm, s1, s2, s3, mine_ref, line_ref, pair_ref, dens_ref, d_ref, half_ref, sems
):
    me = lax.axis_index("mu")
    c = me // 2
    k = me % 2
    size = d_ref.shape[1]
    copies = [
        pltpu.make_async_copy(pair_hbm, pair_ref, sems.at[0]),
        pltpu.make_async_copy(dens_hbm, dens_ref, sems.at[1]),
        pltpu.make_async_copy(d_hbm, d_ref, sems.at[2]),
    ]
    pieces = []
    for i, (send, d) in enumerate(((s1, 1 + k), (s2, 2 - k), (s3, 3))):
        first = (c ^ d) * GROUP
        pieces.append((send, 0, 2, first + 2 * k, c))
        pieces.append((half_ref, 2 * i, 2, first + 2 * (1 - k), c))
        if send is not s3:
            pieces.append((send, 3, GROUP, first, c ^ (3 - d)))
            pieces.append((send, 7, 2, first + 2 * (d - 1), c ^ 3))
    for i, (into, slot, count, first, chip) in enumerate(pieces):
        copies.append(
            pltpu.make_async_copy(
                b_hbm.at[pl.ds(first, count), :, column(chip)], into.at[pl.ds(slot, count)], sems.at[3 + i]
            )
        )
    for copy in copies:
        copy.start()
    copies[0].wait()
    pair_line = expand_row(pair_ref, me, size)
    for j in range(CHIPS):
        line_ref[j] = pair_line[:, j * TILE : (j + 1) * TILE].astype(F32)
    copies[1].wait()
    dens_line = expand_row(dens_ref, me, size)
    copies[2].wait()
    dens = d_ref[...] * dens_line
    mine_ref[...] = dens
    for j in range(CHIPS):
        for send in (s1, s2, s3):
            send[send.shape[0] - CHIPS + j] = dens[:, j * TILE : (j + 1) * TILE]
    for copy, (into, slot, count, first, chip) in zip(copies[3:], pieces):
        copy.wait()
        line = line_ref[chip].astype(BF)
        for p in range(slot, slot + count):
            into[p] = into[p] * line
    for core in (0, 1):

        @pl.when(k == core)
        def _():
            for i, send in enumerate((s1, s2, s3)):
                left, right = (half_ref[2 * i + j][:, core * BLK : (core + 1) * BLK] for j in (0, 1))
                send[2] = jnp.concatenate([left, right], axis=1)


def own_kernel(b_hbm, mine_ref, line_ref, own_ref, sem):
    c = lax.axis_index("mu") // 2
    copy = pltpu.make_async_copy(b_hbm.at[pl.ds(c * GROUP, GROUP)], own_ref.at[pl.ds(0, GROUP)], sem)
    copy.start()
    own_ref[GROUP] = mine_ref[...]
    copy.wait()
    for p in range(GROUP):
        for j in range(CHIPS):
            at = slice(j * TILE, (j + 1) * TILE)
            own_ref[p, :, at] = own_ref[p, :, at] * line_ref[j].astype(BF)


def row_at(p, chip, core):
    return pl.ds(pl.multiple_of(p * 2 * CHIPS * BLK + chip * TILE + core * BLK, BLK), BLK)


def square(p, b0, b1):
    if p < 2:
        corner = b0[p].T[BLK:]
        return b0[p], jnp.concatenate([corner, b1[2][:, p * BLK : (p + 1) * BLK]], axis=1)
    corner = b1[p - 2].T[:BLK]
    return jnp.concatenate([b0[2][:, (p - 2) * BLK : (p - 1) * BLK], corner], axis=1), b1[p - 2]


def early_kernel(own_ref, mate_ref, r1, r2, q1, q2, t_ref, l_ref, x_ref, d_scr, l_scr):
    me = lax.axis_index("mu")
    c = me // 2
    k = me % 2
    size = t_ref.shape[1]
    cx, cy, cg = c ^ 1, c ^ 2, c ^ 3

    def fill(o0, o1, x0, y0, x1, y1):
        for core, own, x, y in ((0, o0, x0, y0), (1, o1, x1, y1)):
            d_scr[row_at(0, c, core), :] = own[GROUP]
            for r, ref in ((cx, x), (cy, y)):
                for j in range(CHIPS):
                    d_scr[row_at(0, r, core), j * TILE : (j + 1) * TILE] = ref[NEAR - CHIPS + j]
            d_scr[row_at(0, cg, core), :] = jnp.zeros((BLK, size), BF)
            for p in range(GROUP):
                t_ref[row_at(p, c, core), :] = own[p]
                t_ref[row_at(p, cx, core), column(cg)] = x[3 + p]
                t_ref[row_at(p, cy, core), column(cg)] = y[3 + p]
                t_ref[row_at(p, cg, core), column(cg)] = jnp.zeros((BLK, TILE), BF)
                if p < 2:
                    t_ref[row_at(p, cx, core), column(cy)] = x[7 + p]
                else:
                    t_ref[row_at(p, cy, core), column(cx)] = y[5 + p]
        for p in range(GROUP):
            for r, b0, b1 in ((cx, x0, x1), (cy, y0, y1)):
                top, low = square(p, b0, b1)
                t_ref[row_at(p, r, 0), column(r)] = top
                t_ref[row_at(p, r, 1), column(r)] = low
            tasks = [(c, dst, o0[p, :, column(dst)], o1[p, :, column(dst)]) for dst in (cx, cy, cg)]
            tasks.append((cx, cg, x0[3 + p], x1[3 + p]))
            tasks.append((cy, cg, y0[3 + p], y1[3 + p]))
            if p < 2:
                tasks.append((cx, cy, x0[7 + p], x1[7 + p]))
            else:
                tasks.append((cy, cx, y0[5 + p], y1[5 + p]))
            for src, dst, top, low in tasks:
                block = jnp.concatenate([top, low], axis=0).T
                t_ref[row_at(p, dst, 0), column(src)] = block[:BLK]
                t_ref[row_at(p, dst, 1), column(src)] = block[BLK:]

    @pl.when(k == 0)
    def _():
        fill(own_ref, mate_ref, r1, r2, q2, q1)

    @pl.when(k == 1)
    def _():
        fill(mate_ref, own_ref, q1, q2, r2, r1)

    for p in range(GROUP):
        for r in range(CHIPS):
            at = slice((p * CHIPS + r) * BLK, (p * CHIPS + r + 1) * BLK)
            l_scr[at, :] = t_ref[row_at(p, r, k), :]
            l_ref[at, :] = t_ref[row_at(p, r, k), column(cg)]
    x_ref[...] = jnp.dot(l_scr[...], d_scr[...], preferred_element_type=F32)


def late_kernel(t_ref, l_ref, xp_ref, r3, q3, e1, e2, e3, keep_ref, d_scr, l_scr, g_scr, x_scr, xg_scr, k_scr):
    me = lax.axis_index("mu")
    c = me // 2
    k = me % 2
    size = t_ref.shape[1]
    half = size // 2
    cg = c ^ 3

    def fill(g0, g1):
        for core, g in ((0, g0), (1, g1)):
            for j in range(CHIPS):
                d_scr[core * BLK : (core + 1) * BLK, j * TILE : (j + 1) * TILE] = g[FAR - CHIPS + j]
        for p in range(GROUP):
            top, low = square(p, g0, g1)
            g_scr[p * TILE : p * TILE + BLK, :] = top
            g_scr[p * TILE + BLK : (p + 1) * TILE, :] = low

    @pl.when(k == 0)
    def _():
        fill(r3, q3)

    @pl.when(k == 1)
    def _():
        fill(q3, r3)

    l_scr[...] = l_ref[...]
    for p in range(GROUP):
        at = pl.ds(pl.multiple_of((p * CHIPS + cg) * BLK, BLK), BLK)
        l_scr[at, :] = g_scr[pl.ds(pl.multiple_of(p * TILE + k * BLK, BLK), BLK), :]
    for p in range(GROUP):
        rest = jnp.dot(l_scr[p * half : (p + 1) * half, :], d_scr[...], preferred_element_type=F32)
        x_scr[:, p * size : (p + 1) * size] = (xp_ref[p * half : (p + 1) * half, :] + rest).astype(BF)
        xg_scr[:, p * TILE : (p + 1) * TILE] = x_scr[:, pl.ds(pl.multiple_of(p * size + cg * TILE, TILE), TILE)]
    k_scr[...] = jnp.dot(x_scr[...], t_ref[...], preferred_element_type=F32)
    k_scr[:, column(cg)] += jnp.dot(xg_scr[...], g_scr[...], preferred_element_type=F32)

    @pl.when(k != Z_FIRST)
    def _():
        for out, step in zip((e1, e2, e3), PLANE_ONE):
            out[...] = k_scr[pl.ds(pl.multiple_of(goal(step, c) * BLK, BLK), BLK), :].astype(BF)
        keep_ref[...] = k_scr[pl.ds(pl.multiple_of(c * BLK, BLK), BLK), :]

    @pl.when(k == Z_FIRST)
    def _():
        a = lax.axis_index("aux")
        for r in range(CHIPS):
            into = slice(r * STRIP, (r + 1) * STRIP)
            for out, step in zip((e1, e2, e3), ALONG_ONE):
                at = pl.ds(pl.multiple_of(r * BLK + goal(step, a) * STRIP, STRIP), STRIP)
                out[into, :] = k_scr[at, :].astype(BF)
            keep_ref[into, :] = k_scr[pl.ds(pl.multiple_of(r * BLK + a * STRIP, STRIP), STRIP), :]


def goal(step, place):
    return sum(jnp.where(place == i, j, 0) for i, j in enumerate(step))


def spread(b_tensor, density, pair_mask, dens_mask):
    width, size = density.shape
    vmem = pl.BlockSpec(memory_space=pltpu.VMEM)
    hbm = pl.BlockSpec(memory_space=pl.ANY)

    def swap(x, step):
        return lax.ppermute(x, "mu", [(i, i ^ step) for i in range(2 * CHIPS)])

    def turn(x, first):
        return lax.ppermute(x, "mu", [(i, i ^ (2 if (i % 2 == 0) == first else 4)) for i in range(2 * CHIPS)])

    def around(x1, x2, x3):
        return turn(x1, True), turn(x2, False), swap(x3, 6)

    def slots(count):
        return jax.ShapeDtypeStruct((count, width, TILE), BF)

    b_tensor, density, pair_mask, dens_mask = (
        pltpu.with_memory_space_constraint(x, pltpu.HBM) for x in (b_tensor, density, pair_mask, dens_mask)
    )
    *sends, mine, line = pl.pallas_call(
        pack_kernel,
        out_shape=[
            slots(NEAR),
            slots(NEAR),
            slots(FAR),
            jax.ShapeDtypeStruct((width, size), BF),
            jax.ShapeDtypeStruct((CHIPS, 1, TILE), F32),
        ],
        in_specs=[hbm] * 4,
        out_specs=[vmem] * 5,
        scratch_shapes=[
            pltpu.SMEM(pair_mask.shape, jnp.int32),
            pltpu.SMEM(dens_mask.shape, jnp.int32),
            pltpu.VMEM(density.shape, BF),
            pltpu.VMEM((6, width, TILE), BF),
            pltpu.SemaphoreType.DMA((13,)),
        ],
        compiler_params=pltpu.CompilerParams(vmem_limit_bytes=16 << 20),
        name="pack",
    )(b_tensor, density, pair_mask, dens_mask)
    own = pl.pallas_call(
        own_kernel,
        out_shape=jax.ShapeDtypeStruct((GROUP + 1, width, size), BF),
        in_specs=[hbm, vmem, vmem],
        out_specs=vmem,
        scratch_shapes=[pltpu.SemaphoreType.DMA],
        compiler_params=pltpu.CompilerParams(vmem_limit_bytes=16 << 20),
        name="own",
    )(b_tensor, mine, line)
    r1, r2, r3 = around(*sends)
    mate = swap(own, 1)
    q1, q2, q3 = swap(r1, 1), swap(r2, 1), swap(r3, 1)
    half = size // 2
    early = pl.pallas_call(
        early_kernel,
        out_shape=[
            jax.ShapeDtypeStruct((GROUP * size, size), BF),
            jax.ShapeDtypeStruct((GROUP * half, TILE), BF),
            jax.ShapeDtypeStruct((GROUP * half, size), F32),
        ],
        in_specs=[vmem] * 6,
        out_specs=[vmem] * 3,
        scratch_shapes=[pltpu.VMEM((size, size), BF), pltpu.VMEM((GROUP * half, size), BF)],
        compiler_params=pltpu.CompilerParams(vmem_limit_bytes=32 << 20),
        name="early",
    )(own, mate, r1, r2, q1, q2)
    chunk = jax.ShapeDtypeStruct((width, size), BF)
    *parts, keep = pl.pallas_call(
        late_kernel,
        out_shape=[chunk, chunk, chunk, jax.ShapeDtypeStruct((width, size), F32)],
        in_specs=[vmem] * 5,
        out_specs=[vmem] * 4,
        scratch_shapes=[
            pltpu.VMEM((TILE, size), BF),
            pltpu.VMEM((GROUP * half, TILE), BF),
            pltpu.VMEM((GROUP * TILE, TILE), BF),
            pltpu.VMEM((half, GROUP * size), BF),
            pltpu.VMEM((half, GROUP * TILE), BF),
            pltpu.VMEM((half, size), F32),
        ],
        compiler_params=pltpu.CompilerParams(vmem_limit_bytes=32 << 20),
        name="late",
    )(*early, r3, q3)

    def cross(x, plane, along, z_core):
        pairs = []
        for i in range(2 * CHIPS * LAYERS):
            mu, a = divmod(i, LAYERS)
            c, k = divmod(mu, 2)
            if k == z_core:
                pairs.append((i, mu * LAYERS + along[a]))
            else:
                pairs.append((i, (2 * plane[c] + k) * LAYERS + a))
        return lax.ppermute(x, ("mu", "aux"), pairs)

    once = keep
    for part, plane, along in zip(parts, PLANE_ONE, ALONG_ONE):
        once = once + cross(part, plane, along, Z_FIRST).astype(F32)
    once = once.reshape(CHIPS, STRIP, size)
    me = lax.axis_index("mu")
    z_now = me % 2 != Z_FIRST
    c, a = me // 2, lax.axis_index("aux")

    def strip_of(index):
        return lax.dynamic_index_in_dim(once, index, 0, keepdims=False)

    total = strip_of(jnp.where(z_now, a, c))
    for plane, along in zip(PLANE_TWO, ALONG_TWO):
        to = jnp.where(z_now, goal(along, a), goal(plane, c))
        total = total + cross(strip_of(to), plane, along, 1 - Z_FIRST)
    return total


def gathered(b_tensor, density, pair_mask, dens_mask):
    depth, width, nbas = b_tensor.shape
    owner = lax.axis_index("mu")
    pair_row = lax.dynamic_slice_in_dim(pair_mask, owner, 1, 0)[0]
    dens_row = lax.dynamic_slice_in_dim(dens_mask, owner, 1, 0)[0]
    kept = b_tensor * jnp.repeat(pair_row, width).astype(BF)[None, None, :]
    dens_kept = density * jnp.repeat(dens_row, width).astype(BF)[None, :]
    summed = jnp.dot(
        kept.reshape(depth * width, nbas),
        lax.all_gather(dens_kept, "mu", axis=0, tiled=True),
        preferred_element_type=F32,
    )
    half_x = summed.astype(BF).reshape(depth, width, nbas)
    x_cols = lax.all_to_all(half_x, "mu", split_axis=2, concat_axis=1, tiled=True)
    partner = lax.all_to_all(kept, "mu", split_axis=2, concat_axis=1, tiled=True)
    return lax.psum_scatter(
        jnp.einsum("pms,pns->mn", x_cols, partner, preferred_element_type=F32),
        ("mu", "aux"),
        scatter_dimension=0,
        tiled=True,
    )


def solution(mesh):
    in_specs = (P("aux", "mu", None), P("mu", None), P(), P())
    out_specs = P(("mu", "aux"), None)

    def per_device(b_tensor, density, pair_mask, dens_mask):
        depth, width, size = b_tensor.shape
        fits = mesh.shape["mu"] == 2 * CHIPS and mesh.shape["aux"] == LAYERS
        fits = fits and depth == GROUP * CHIPS and width == BLK and size == 2 * CHIPS * BLK
        step = spread if fits else gathered
        return step(b_tensor, density, pair_mask, dens_mask)

    return jax.shard_map(per_device, mesh=mesh, in_specs=in_specs, out_specs=out_specs, check_vma=False)
```

```python
import jax
import jax.numpy as jnp
from jax import lax
from jax.experimental import pallas as pl
from jax.experimental.pallas import tpu as pltpu
from jax.sharding import PartitionSpec as P

BF = jnp.bfloat16
F32 = jnp.float32
BLK = 64
TILE = 2 * BLK
CHIPS = 4
GROUP = 4
STEPS = ((2, 3, 1, 0), (3, 2, 0, 1), (1, 0, 3, 2))
NEAR = 13
FAR = 7


def expand_row(mask_ref, row, size):
    block = lax.broadcasted_iota(jnp.int32, (1, size), 1) // BLK
    line = jnp.zeros((1, size), F32)
    for j in range(size // BLK):
        line = jnp.where(block == j, mask_ref[row, j].astype(F32), line)
    return line.astype(BF)


def column(chip):
    return pl.ds(pl.multiple_of(chip * TILE, TILE), TILE)


def pack_kernel(
    b_hbm, d_hbm, pair_hbm, dens_hbm, own_ref, s1, s2, s3, pair_ref, dens_ref, d_ref, half_ref, line_ref, sems
):
    me = lax.axis_index("mu")
    c = me // 2
    k = me % 2
    size = d_ref.shape[1]
    copies = [
        pltpu.make_async_copy(pair_hbm, pair_ref, sems.at[0]),
        pltpu.make_async_copy(dens_hbm, dens_ref, sems.at[1]),
        pltpu.make_async_copy(d_hbm, d_ref, sems.at[2]),
    ]
    pieces = []
    for i, (send, d) in enumerate(((s1, 1 + k), (s2, 2 - k), (s3, 3))):
        first = (c ^ d) * GROUP
        pieces.append((send, 0, 2, first + 2 * k, c))
        pieces.append((half_ref, 2 * i, 2, first + 2 * (1 - k), c))
        if send is not s3:
            pieces.append((send, 3, GROUP, first, c ^ (3 - d)))
            pieces.append((send, 7, 2, first + 2 * (d - 1), c ^ 3))
    for i, (into, slot, count, first, chip) in enumerate(pieces):
        copies.append(
            pltpu.make_async_copy(
                b_hbm.at[pl.ds(first, count), :, column(chip)], into.at[pl.ds(slot, count)], sems.at[3 + i]
            )
        )
    copies.append(
        pltpu.make_async_copy(b_hbm.at[pl.ds(c * GROUP, GROUP)], own_ref.at[pl.ds(0, GROUP)], sems.at[3 + len(pieces)])
    )
    for copy in copies:
        copy.start()
    copies[0].wait()
    pair_line = expand_row(pair_ref, me, size)
    for j in range(CHIPS):
        line_ref[j] = pair_line[:, j * TILE : (j + 1) * TILE].astype(F32)
    copies[1].wait()
    dens_line = expand_row(dens_ref, me, size)
    copies[2].wait()
    dens = d_ref[...] * dens_line
    own_ref[GROUP] = dens
    for j in range(CHIPS):
        for send in (s1, s2, s3):
            send[send.shape[0] - CHIPS + j] = dens[:, j * TILE : (j + 1) * TILE]
    for copy, (into, slot, count, first, chip) in zip(copies[3:], pieces):
        copy.wait()
        line = line_ref[chip].astype(BF)
        for p in range(slot, slot + count):
            into[p] = into[p] * line
    for core in (0, 1):

        @pl.when(k == core)
        def _():
            for i, send in enumerate((s1, s2, s3)):
                left, right = (half_ref[2 * i + j][:, core * BLK : (core + 1) * BLK] for j in (0, 1))
                send[2] = jnp.concatenate([left, right], axis=1)

    copies[-1].wait()
    for p in range(GROUP):
        own_ref[p] = own_ref[p] * pair_line


def row_at(p, chip, core):
    return pl.ds(pl.multiple_of(p * 2 * CHIPS * BLK + chip * TILE + core * BLK, BLK), BLK)


def square(p, b0, b1):
    if p < 2:
        corner = b0[p].T[BLK:]
        return b0[p], jnp.concatenate([corner, b1[2][:, p * BLK : (p + 1) * BLK]], axis=1)
    corner = b1[p - 2].T[:BLK]
    return jnp.concatenate([b0[2][:, (p - 2) * BLK : (p - 1) * BLK], corner], axis=1), b1[p - 2]


def early_kernel(own_ref, mate_ref, r1, r2, q1, q2, t_ref, l_ref, x_ref, d_scr, l_scr):
    me = lax.axis_index("mu")
    c = me // 2
    k = me % 2
    size = t_ref.shape[1]
    cx, cy, cg = c ^ 1, c ^ 2, c ^ 3

    def fill(o0, o1, x0, y0, x1, y1):
        for core, own, x, y in ((0, o0, x0, y0), (1, o1, x1, y1)):
            d_scr[row_at(0, c, core), :] = own[GROUP]
            for r, ref in ((cx, x), (cy, y)):
                for j in range(CHIPS):
                    d_scr[row_at(0, r, core), j * TILE : (j + 1) * TILE] = ref[NEAR - CHIPS + j]
            d_scr[row_at(0, cg, core), :] = jnp.zeros((BLK, size), BF)
            for p in range(GROUP):
                t_ref[row_at(p, c, core), :] = own[p]
                t_ref[row_at(p, cx, core), column(cg)] = x[3 + p]
                t_ref[row_at(p, cy, core), column(cg)] = y[3 + p]
                t_ref[row_at(p, cg, core), column(cg)] = jnp.zeros((BLK, TILE), BF)
                if p < 2:
                    t_ref[row_at(p, cx, core), column(cy)] = x[7 + p]
                else:
                    t_ref[row_at(p, cy, core), column(cx)] = y[5 + p]
        for p in range(GROUP):
            for r, b0, b1 in ((cx, x0, x1), (cy, y0, y1)):
                top, low = square(p, b0, b1)
                t_ref[row_at(p, r, 0), column(r)] = top
                t_ref[row_at(p, r, 1), column(r)] = low
            tasks = [(c, dst, o0[p, :, column(dst)], o1[p, :, column(dst)]) for dst in (cx, cy, cg)]
            tasks.append((cx, cg, x0[3 + p], x1[3 + p]))
            tasks.append((cy, cg, y0[3 + p], y1[3 + p]))
            if p < 2:
                tasks.append((cx, cy, x0[7 + p], x1[7 + p]))
            else:
                tasks.append((cy, cx, y0[5 + p], y1[5 + p]))
            for src, dst, top, low in tasks:
                block = jnp.concatenate([top, low], axis=0).T
                t_ref[row_at(p, dst, 0), column(src)] = block[:BLK]
                t_ref[row_at(p, dst, 1), column(src)] = block[BLK:]

    @pl.when(k == 0)
    def _():
        fill(own_ref, mate_ref, r1, r2, q2, q1)

    @pl.when(k == 1)
    def _():
        fill(mate_ref, own_ref, q1, q2, r2, r1)

    for p in range(GROUP):
        for r in range(CHIPS):
            at = slice((p * CHIPS + r) * BLK, (p * CHIPS + r + 1) * BLK)
            l_scr[at, :] = t_ref[row_at(p, r, k), :]
            l_ref[at, :] = t_ref[row_at(p, r, k), column(cg)]
    x_ref[...] = jnp.dot(l_scr[...], d_scr[...], preferred_element_type=F32)


def late_kernel(t_ref, l_ref, xp_ref, r3, q3, e1, e2, e3, keep_ref, d_scr, l_scr, g_scr, x_scr, xg_scr, k_scr):
    me = lax.axis_index("mu")
    c = me // 2
    k = me % 2
    size = t_ref.shape[1]
    half = size // 2
    cg = c ^ 3

    def fill(g0, g1):
        for core, g in ((0, g0), (1, g1)):
            for j in range(CHIPS):
                d_scr[core * BLK : (core + 1) * BLK, j * TILE : (j + 1) * TILE] = g[FAR - CHIPS + j]
        for p in range(GROUP):
            top, low = square(p, g0, g1)
            g_scr[p * TILE : p * TILE + BLK, :] = top
            g_scr[p * TILE + BLK : (p + 1) * TILE, :] = low

    @pl.when(k == 0)
    def _():
        fill(r3, q3)

    @pl.when(k == 1)
    def _():
        fill(q3, r3)

    l_scr[...] = l_ref[...]
    for p in range(GROUP):
        at = pl.ds(pl.multiple_of((p * CHIPS + cg) * BLK, BLK), BLK)
        l_scr[at, :] = g_scr[pl.ds(pl.multiple_of(p * TILE + k * BLK, BLK), BLK), :]
    for p in range(GROUP):
        rest = jnp.dot(l_scr[p * half : (p + 1) * half, :], d_scr[...], preferred_element_type=F32)
        x_scr[:, p * size : (p + 1) * size] = (xp_ref[p * half : (p + 1) * half, :] + rest).astype(BF)
        xg_scr[:, p * TILE : (p + 1) * TILE] = x_scr[:, pl.ds(pl.multiple_of(p * size + cg * TILE, TILE), TILE)]
    corner = jnp.dot(xg_scr[...], g_scr[...], preferred_element_type=F32)
    k_scr[...] = jnp.dot(x_scr[...], t_ref[...], preferred_element_type=F32)
    k_scr[:, column(cg)] += corner
    for out, d in ((e1, 1 + k), (e2, 2 - k), (e3, 3)):
        out[...] = k_scr[pl.ds(pl.multiple_of((c ^ d) * BLK, BLK), BLK), :].astype(BF)
    keep_ref[...] = k_scr[pl.ds(pl.multiple_of(c * BLK, BLK), BLK), :]


def spread(b_tensor, density, pair_mask, dens_mask):
    width, size = density.shape
    vmem = pl.BlockSpec(memory_space=pltpu.VMEM)
    hbm = pl.BlockSpec(memory_space=pl.ANY)

    def swap(x, step):
        return lax.ppermute(x, "mu", [(i, i ^ step) for i in range(2 * CHIPS)])

    def turn(x, first):
        return lax.ppermute(x, "mu", [(i, i ^ (2 if (i % 2 == 0) == first else 4)) for i in range(2 * CHIPS)])

    def around(x1, x2, x3):
        return turn(x1, True), turn(x2, False), swap(x3, 6)

    def slots(count):
        return jax.ShapeDtypeStruct((count, width, TILE), BF)

    own, *sends = pl.pallas_call(
        pack_kernel,
        out_shape=[jax.ShapeDtypeStruct((GROUP + 1, width, size), BF), slots(NEAR), slots(NEAR), slots(FAR)],
        in_specs=[hbm] * 4,
        out_specs=[vmem] * 4,
        scratch_shapes=[
            pltpu.SMEM(pair_mask.shape, jnp.int32),
            pltpu.SMEM(dens_mask.shape, jnp.int32),
            pltpu.VMEM(density.shape, BF),
            pltpu.VMEM((6, width, TILE), BF),
            pltpu.VMEM((CHIPS, 1, TILE), F32),
            pltpu.SemaphoreType.DMA((14,)),
        ],
        compiler_params=pltpu.CompilerParams(vmem_limit_bytes=16 << 20),
        name="pack",
    )(*(pltpu.with_memory_space_constraint(x, pltpu.HBM) for x in (b_tensor, density, pair_mask, dens_mask)))
    r1, r2, r3 = around(*sends)
    mate = swap(own, 1)
    q1, q2, q3 = swap(r1, 1), swap(r2, 1), swap(r3, 1)
    half = size // 2
    early = pl.pallas_call(
        early_kernel,
        out_shape=[
            jax.ShapeDtypeStruct((GROUP * size, size), BF),
            jax.ShapeDtypeStruct((GROUP * half, TILE), BF),
            jax.ShapeDtypeStruct((GROUP * half, size), F32),
        ],
        in_specs=[vmem] * 6,
        out_specs=[vmem] * 3,
        scratch_shapes=[pltpu.VMEM((size, size), BF), pltpu.VMEM((GROUP * half, size), BF)],
        compiler_params=pltpu.CompilerParams(vmem_limit_bytes=32 << 20),
        name="early",
    )(own, mate, r1, r2, q1, q2)
    chunk = jax.ShapeDtypeStruct((width, size), BF)
    *parts, keep = pl.pallas_call(
        late_kernel,
        out_shape=[chunk, chunk, chunk, jax.ShapeDtypeStruct((width, size), F32)],
        in_specs=[vmem] * 5,
        out_specs=[vmem] * 4,
        scratch_shapes=[
            pltpu.VMEM((TILE, size), BF),
            pltpu.VMEM((GROUP * half, TILE), BF),
            pltpu.VMEM((GROUP * TILE, TILE), BF),
            pltpu.VMEM((half, GROUP * size), BF),
            pltpu.VMEM((half, GROUP * TILE), BF),
            pltpu.VMEM((half, size), F32),
        ],
        compiler_params=pltpu.CompilerParams(vmem_limit_bytes=32 << 20),
        name="late",
    )(*early, r3, q3)
    y1, y2, y3 = around(*parts)
    plane = (((keep + y3.astype(F32)) + y1.astype(F32)) + y2.astype(F32))
    a = lax.axis_index("aux")
    strip = width // 4

    def strip_of(index):
        return lax.dynamic_slice_in_dim(plane, index * strip, strip, 0)

    total = strip_of(a)
    for step in STEPS:
        to = sum(jnp.where(a == i, j, 0) for i, j in enumerate(step))
        total = total + lax.ppermute(strip_of(to), "aux", list(enumerate(step)))
    return total


def gathered(b_tensor, density, pair_mask, dens_mask):
    depth, width, nbas = b_tensor.shape
    owner = lax.axis_index("mu")
    pair_row = lax.dynamic_slice_in_dim(pair_mask, owner, 1, 0)[0]
    dens_row = lax.dynamic_slice_in_dim(dens_mask, owner, 1, 0)[0]
    kept = b_tensor * jnp.repeat(pair_row, width).astype(BF)[None, None, :]
    dens_kept = density * jnp.repeat(dens_row, width).astype(BF)[None, :]
    summed = jnp.dot(
        kept.reshape(depth * width, nbas),
        lax.all_gather(dens_kept, "mu", axis=0, tiled=True),
        preferred_element_type=F32,
    )
    half_x = summed.astype(BF).reshape(depth, width, nbas)
    x_cols = lax.all_to_all(half_x, "mu", split_axis=2, concat_axis=1, tiled=True)
    partner = lax.all_to_all(kept, "mu", split_axis=2, concat_axis=1, tiled=True)
    return lax.psum_scatter(
        jnp.einsum("pms,pns->mn", x_cols, partner, preferred_element_type=F32),
        ("mu", "aux"),
        scatter_dimension=0,
        tiled=True,
    )


def solution(mesh):
    in_specs = (P("aux", "mu", None), P("mu", None), P(), P())
    out_specs = P(("mu", "aux"), None)

    def per_device(b_tensor, density, pair_mask, dens_mask):
        depth, width, size = b_tensor.shape
        fits = mesh.shape["mu"] == 2 * CHIPS and mesh.shape["aux"] == 4
        fits = fits and depth == GROUP * CHIPS and width == BLK and size == 2 * CHIPS * BLK
        step = spread if fits else gathered
        return step(b_tensor, density, pair_mask, dens_mask)

    return jax.shard_map(per_device, mesh=mesh, in_specs=in_specs, out_specs=out_specs, check_vma=False)
```

```python
import jax
import jax.numpy as jnp
from jax import lax
from jax.experimental import pallas as pl
from jax.experimental.pallas import tpu as pltpu
from jax.sharding import PartitionSpec as P

BF = jnp.bfloat16
F32 = jnp.float32
BLK = 64
TILE = 2 * BLK
CHIPS = 4
GROUP = 4
PLANE = ((3, 2, 1, 0), (1, 3, 0, 2), (2, 0, 3, 1))
STEPS = ((2, 3, 1, 0), (3, 2, 0, 1), (1, 0, 3, 2))
NEAR = 13
FAR = 7


def expand_row(mask_ref, row, size):
    block = lax.broadcasted_iota(jnp.int32, (1, size), 1) // BLK
    line = jnp.zeros((1, size), F32)
    for j in range(size // BLK):
        line = jnp.where(block == j, mask_ref[row, j].astype(F32), line)
    return line.astype(BF)


def column(chip):
    return pl.ds(pl.multiple_of(chip * TILE, TILE), TILE)


def pack_kernel(
    b_hbm, d_hbm, pair_hbm, dens_hbm, s1, s2, s3, mine_ref, line_ref, pair_ref, dens_ref, d_ref, half_ref, sems
):
    me = lax.axis_index("mu")
    c = me // 2
    k = me % 2
    size = d_ref.shape[1]
    copies = [
        pltpu.make_async_copy(pair_hbm, pair_ref, sems.at[0]),
        pltpu.make_async_copy(dens_hbm, dens_ref, sems.at[1]),
        pltpu.make_async_copy(d_hbm, d_ref, sems.at[2]),
    ]
    pieces = []
    for i, (send, d) in enumerate(((s1, 1 + k), (s2, 2 - k), (s3, 3))):
        first = (c ^ d) * GROUP
        pieces.append((send, 0, 2, first + 2 * k, c))
        pieces.append((half_ref, 2 * i, 2, first + 2 * (1 - k), c))
        if send is not s3:
            pieces.append((send, 3, GROUP, first, c ^ (3 - d)))
            pieces.append((send, 7, 2, first + 2 * (d - 1), c ^ 3))
    for i, (into, slot, count, first, chip) in enumerate(pieces):
        copies.append(
            pltpu.make_async_copy(
                b_hbm.at[pl.ds(first, count), :, column(chip)], into.at[pl.ds(slot, count)], sems.at[3 + i]
            )
        )
    for copy in copies:
        copy.start()
    copies[0].wait()
    pair_line = expand_row(pair_ref, me, size)
    for j in range(CHIPS):
        line_ref[j] = pair_line[:, j * TILE : (j + 1) * TILE].astype(F32)
    copies[1].wait()
    dens_line = expand_row(dens_ref, me, size)
    copies[2].wait()
    dens = d_ref[...] * dens_line
    mine_ref[...] = dens
    for j in range(CHIPS):
        for send in (s1, s2, s3):
            send[send.shape[0] - CHIPS + j] = dens[:, j * TILE : (j + 1) * TILE]
    for copy, (into, slot, count, first, chip) in zip(copies[3:], pieces):
        copy.wait()
        line = line_ref[chip].astype(BF)
        for p in range(slot, slot + count):
            into[p] = into[p] * line
    for core in (0, 1):

        @pl.when(k == core)
        def _():
            for i, send in enumerate((s1, s2, s3)):
                left, right = (half_ref[2 * i + j][:, core * BLK : (core + 1) * BLK] for j in (0, 1))
                send[2] = jnp.concatenate([left, right], axis=1)


def own_kernel(b_hbm, mine_ref, line_ref, own_ref, sem):
    c = lax.axis_index("mu") // 2
    copy = pltpu.make_async_copy(b_hbm.at[pl.ds(c * GROUP, GROUP)], own_ref.at[pl.ds(0, GROUP)], sem)
    copy.start()
    own_ref[GROUP] = mine_ref[...]
    copy.wait()
    for p in range(GROUP):
        for j in range(CHIPS):
            at = slice(j * TILE, (j + 1) * TILE)
            own_ref[p, :, at] = own_ref[p, :, at] * line_ref[j].astype(BF)


def row_at(p, chip, core):
    return pl.ds(pl.multiple_of(p * 2 * CHIPS * BLK + chip * TILE + core * BLK, BLK), BLK)


def square(p, b0, b1):
    if p < 2:
        corner = b0[p].T[BLK:]
        return b0[p], jnp.concatenate([corner, b1[2][:, p * BLK : (p + 1) * BLK]], axis=1)
    corner = b1[p - 2].T[:BLK]
    return jnp.concatenate([b0[2][:, (p - 2) * BLK : (p - 1) * BLK], corner], axis=1), b1[p - 2]


def early_kernel(own_ref, mate_ref, r1, r2, q1, q2, t_ref, l_ref, x_ref, d_scr, l_scr):
    me = lax.axis_index("mu")
    c = me // 2
    k = me % 2
    size = t_ref.shape[1]
    cx, cy, cg = c ^ 1, c ^ 2, c ^ 3

    def fill(o0, o1, x0, y0, x1, y1):
        for core, own, x, y in ((0, o0, x0, y0), (1, o1, x1, y1)):
            d_scr[row_at(0, c, core), :] = own[GROUP]
            for r, ref in ((cx, x), (cy, y)):
                for j in range(CHIPS):
                    d_scr[row_at(0, r, core), j * TILE : (j + 1) * TILE] = ref[NEAR - CHIPS + j]
            d_scr[row_at(0, cg, core), :] = jnp.zeros((BLK, size), BF)
            for p in range(GROUP):
                t_ref[row_at(p, c, core), :] = own[p]
                t_ref[row_at(p, cx, core), column(cg)] = x[3 + p]
                t_ref[row_at(p, cy, core), column(cg)] = y[3 + p]
                t_ref[row_at(p, cg, core), column(cg)] = jnp.zeros((BLK, TILE), BF)
                if p < 2:
                    t_ref[row_at(p, cx, core), column(cy)] = x[7 + p]
                else:
                    t_ref[row_at(p, cy, core), column(cx)] = y[5 + p]
        for p in range(GROUP):
            for r, b0, b1 in ((cx, x0, x1), (cy, y0, y1)):
                top, low = square(p, b0, b1)
                t_ref[row_at(p, r, 0), column(r)] = top
                t_ref[row_at(p, r, 1), column(r)] = low
            tasks = [(c, dst, o0[p, :, column(dst)], o1[p, :, column(dst)]) for dst in (cx, cy, cg)]
            tasks.append((cx, cg, x0[3 + p], x1[3 + p]))
            tasks.append((cy, cg, y0[3 + p], y1[3 + p]))
            if p < 2:
                tasks.append((cx, cy, x0[7 + p], x1[7 + p]))
            else:
                tasks.append((cy, cx, y0[5 + p], y1[5 + p]))
            for src, dst, top, low in tasks:
                block = jnp.concatenate([top, low], axis=0).T
                t_ref[row_at(p, dst, 0), column(src)] = block[:BLK]
                t_ref[row_at(p, dst, 1), column(src)] = block[BLK:]

    @pl.when(k == 0)
    def _():
        fill(own_ref, mate_ref, r1, r2, q2, q1)

    @pl.when(k == 1)
    def _():
        fill(mate_ref, own_ref, q1, q2, r2, r1)

    for p in range(GROUP):
        for r in range(CHIPS):
            at = slice((p * CHIPS + r) * BLK, (p * CHIPS + r + 1) * BLK)
            l_scr[at, :] = t_ref[row_at(p, r, k), :]
            l_ref[at, :] = t_ref[row_at(p, r, k), column(cg)]
    x_ref[...] = jnp.dot(l_scr[...], d_scr[...], preferred_element_type=F32)


def late_kernel(t_ref, l_ref, xp_ref, r3, q3, e1, e2, e3, keep_ref, d_scr, l_scr, g_scr, x_scr, xg_scr, k_scr):
    me = lax.axis_index("mu")
    c = me // 2
    k = me % 2
    size = t_ref.shape[1]
    half = size // 2
    cg = c ^ 3

    def fill(g0, g1):
        for core, g in ((0, g0), (1, g1)):
            for j in range(CHIPS):
                d_scr[core * BLK : (core + 1) * BLK, j * TILE : (j + 1) * TILE] = g[FAR - CHIPS + j]
        for p in range(GROUP):
            top, low = square(p, g0, g1)
            g_scr[p * TILE : p * TILE + BLK, :] = top
            g_scr[p * TILE + BLK : (p + 1) * TILE, :] = low

    @pl.when(k == 0)
    def _():
        fill(r3, q3)

    @pl.when(k == 1)
    def _():
        fill(q3, r3)

    l_scr[...] = l_ref[...]
    for p in range(GROUP):
        at = pl.ds(pl.multiple_of((p * CHIPS + cg) * BLK, BLK), BLK)
        l_scr[at, :] = g_scr[pl.ds(pl.multiple_of(p * TILE + k * BLK, BLK), BLK), :]
    for p in range(GROUP):
        rest = jnp.dot(l_scr[p * half : (p + 1) * half, :], d_scr[...], preferred_element_type=F32)
        x_scr[:, p * size : (p + 1) * size] = (xp_ref[p * half : (p + 1) * half, :] + rest).astype(BF)
        xg_scr[:, p * TILE : (p + 1) * TILE] = x_scr[:, pl.ds(pl.multiple_of(p * size + cg * TILE, TILE), TILE)]
    k_scr[...] = jnp.dot(x_scr[...], t_ref[...], preferred_element_type=F32)
    k_scr[:, column(cg)] += jnp.dot(xg_scr[...], g_scr[...], preferred_element_type=F32)
    for out, step in zip((e1, e2, e3), PLANE):
        to = sum(jnp.where(c == i, j, 0) for i, j in enumerate(step))
        out[...] = k_scr[pl.ds(pl.multiple_of(to * BLK, BLK), BLK), :].astype(BF)
    keep_ref[...] = k_scr[pl.ds(pl.multiple_of(c * BLK, BLK), BLK), :]


def spread(b_tensor, density, pair_mask, dens_mask):
    width, size = density.shape
    vmem = pl.BlockSpec(memory_space=pltpu.VMEM)
    hbm = pl.BlockSpec(memory_space=pl.ANY)

    def swap(x, step):
        return lax.ppermute(x, "mu", [(i, i ^ step) for i in range(2 * CHIPS)])

    def turn(x, first):
        return lax.ppermute(x, "mu", [(i, i ^ (2 if (i % 2 == 0) == first else 4)) for i in range(2 * CHIPS)])

    def around(x1, x2, x3):
        return turn(x1, True), turn(x2, False), swap(x3, 6)

    def slots(count):
        return jax.ShapeDtypeStruct((count, width, TILE), BF)

    b_tensor, density, pair_mask, dens_mask = (
        pltpu.with_memory_space_constraint(x, pltpu.HBM) for x in (b_tensor, density, pair_mask, dens_mask)
    )
    *sends, mine, line = pl.pallas_call(
        pack_kernel,
        out_shape=[
            slots(NEAR),
            slots(NEAR),
            slots(FAR),
            jax.ShapeDtypeStruct((width, size), BF),
            jax.ShapeDtypeStruct((CHIPS, 1, TILE), F32),
        ],
        in_specs=[hbm] * 4,
        out_specs=[vmem] * 5,
        scratch_shapes=[
            pltpu.SMEM(pair_mask.shape, jnp.int32),
            pltpu.SMEM(dens_mask.shape, jnp.int32),
            pltpu.VMEM(density.shape, BF),
            pltpu.VMEM((6, width, TILE), BF),
            pltpu.SemaphoreType.DMA((13,)),
        ],
        compiler_params=pltpu.CompilerParams(vmem_limit_bytes=16 << 20),
        name="pack",
    )(b_tensor, density, pair_mask, dens_mask)
    own = pl.pallas_call(
        own_kernel,
        out_shape=jax.ShapeDtypeStruct((GROUP + 1, width, size), BF),
        in_specs=[hbm, vmem, vmem],
        out_specs=vmem,
        scratch_shapes=[pltpu.SemaphoreType.DMA],
        compiler_params=pltpu.CompilerParams(vmem_limit_bytes=16 << 20),
        name="own",
    )(b_tensor, mine, line)
    r1, r2, r3 = around(*sends)
    mate = swap(own, 1)
    q1, q2, q3 = swap(r1, 1), swap(r2, 1), swap(r3, 1)
    half = size // 2
    early = pl.pallas_call(
        early_kernel,
        out_shape=[
            jax.ShapeDtypeStruct((GROUP * size, size), BF),
            jax.ShapeDtypeStruct((GROUP * half, TILE), BF),
            jax.ShapeDtypeStruct((GROUP * half, size), F32),
        ],
        in_specs=[vmem] * 6,
        out_specs=[vmem] * 3,
        scratch_shapes=[pltpu.VMEM((size, size), BF), pltpu.VMEM((GROUP * half, size), BF)],
        compiler_params=pltpu.CompilerParams(vmem_limit_bytes=32 << 20),
        name="early",
    )(own, mate, r1, r2, q1, q2)
    chunk = jax.ShapeDtypeStruct((width, size), BF)
    *parts, keep = pl.pallas_call(
        late_kernel,
        out_shape=[chunk, chunk, chunk, jax.ShapeDtypeStruct((width, size), F32)],
        in_specs=[vmem] * 5,
        out_specs=[vmem] * 4,
        scratch_shapes=[
            pltpu.VMEM((TILE, size), BF),
            pltpu.VMEM((GROUP * half, TILE), BF),
            pltpu.VMEM((GROUP * TILE, TILE), BF),
            pltpu.VMEM((half, GROUP * size), BF),
            pltpu.VMEM((half, GROUP * TILE), BF),
            pltpu.VMEM((half, size), F32),
        ],
        compiler_params=pltpu.CompilerParams(vmem_limit_bytes=32 << 20),
        name="late",
    )(*early, r3, q3)
    plane = keep
    for part, step in zip(parts, PLANE):
        pairs = [(2 * i + core, 2 * j + core) for i, j in enumerate(step) for core in (0, 1)]
        plane = plane + lax.ppermute(part, "mu", pairs).astype(F32)
    a = lax.axis_index("aux")
    strip = width // 4

    def strip_of(index):
        return lax.dynamic_slice_in_dim(plane, index * strip, strip, 0)

    total = strip_of(a)
    for step in STEPS:
        to = sum(jnp.where(a == i, j, 0) for i, j in enumerate(step))
        total = total + lax.ppermute(strip_of(to), "aux", list(enumerate(step)))
    return total


def gathered(b_tensor, density, pair_mask, dens_mask):
    depth, width, nbas = b_tensor.shape
    owner = lax.axis_index("mu")
    pair_row = lax.dynamic_slice_in_dim(pair_mask, owner, 1, 0)[0]
    dens_row = lax.dynamic_slice_in_dim(dens_mask, owner, 1, 0)[0]
    kept = b_tensor * jnp.repeat(pair_row, width).astype(BF)[None, None, :]
    dens_kept = density * jnp.repeat(dens_row, width).astype(BF)[None, :]
    summed = jnp.dot(
        kept.reshape(depth * width, nbas),
        lax.all_gather(dens_kept, "mu", axis=0, tiled=True),
        preferred_element_type=F32,
    )
    half_x = summed.astype(BF).reshape(depth, width, nbas)
    x_cols = lax.all_to_all(half_x, "mu", split_axis=2, concat_axis=1, tiled=True)
    partner = lax.all_to_all(kept, "mu", split_axis=2, concat_axis=1, tiled=True)
    return lax.psum_scatter(
        jnp.einsum("pms,pns->mn", x_cols, partner, preferred_element_type=F32),
        ("mu", "aux"),
        scatter_dimension=0,
        tiled=True,
    )


def solution(mesh):
    in_specs = (P("aux", "mu", None), P("mu", None), P(), P())
    out_specs = P(("mu", "aux"), None)

    def per_device(b_tensor, density, pair_mask, dens_mask):
        depth, width, size = b_tensor.shape
        fits = mesh.shape["mu"] == 2 * CHIPS and mesh.shape["aux"] == 4
        fits = fits and depth == GROUP * CHIPS and width == BLK and size == 2 * CHIPS * BLK
        step = spread if fits else gathered
        return step(b_tensor, density, pair_mask, dens_mask)

    return jax.shard_map(per_device, mesh=mesh, in_specs=in_specs, out_specs=out_specs, check_vma=False)
```
